32 devices in a mesh: blk: 16 (over z, y, core), event: 2 (over x).
Axes of the slice: x: 2, y: 2, z: 4, core: 2. Of those that a mesh axis runs over, the one named last changes fastest.
Arguments:
- adjoint_now: float32 [2, 3, 128, 64, 128], P('event', None, 'blk'), may hold values from -6 to 6
- adjoint_prev: float32 [2, 3, 128, 64, 128], P('event', None, 'blk'), may hold values from -6 to 6
- forward_field: float32 [2, 2, 3, 128, 64, 128], P('event', None, None, 'blk'), may hold values from -6 to 6
- density: float32 [128, 64, 128], P('blk'), may hold values from 0.5 to 2
- lame_first: float32 [128, 64, 128], P('blk'), may hold values from 0.5 to 2
- shear_modulus: float32 [128, 64, 128], P('blk'), may hold values from 0.3 to 1.2
Outputs:
- adjoint_field: float32 [2, 3, 128, 64, 128], P('event', None, 'blk')
- shear_kernel: float32 [128, 64, 128], P('blk', 'event')
- bulk_kernel: float32 [128, 64, 128], P('blk', 'event')
The draws below stay inside these ranges and needn't reach their ends.
All inputs are finite; a program needn't handle non-finite values.
Results may differ from the reference program's by a relative error of at most 0.00002.
Values sent between devices are 32-bit elements; how exact they have to be, the bound alone decides.
No kernel may reach another device: no remote copies, remote signals or barrier semaphores. Data moves between devices by JAX's collectives and lax.ppermute only.
A program may use at most 64 MiB of HBM per device.

```python
import math
import jax
import jax.numpy as jnp
from jax import lax

NY = 64
NZ = 128
STEPS = 2
NX = 128
GROUPS = 2


def level_of(rng, shape, split, smallest, high):
    factor_of, own = 1.0, jax.random.fold_in(rng, 6)
    for dim, blocks in split:
        heights = jnp.exp(jax.random.uniform(jax.random.fold_in(own, dim), (blocks,), jnp.float32, smallest / len(split), high / len(split)))
        factor_of = factor_of * jnp.repeat(heights, shape[dim] // blocks).reshape([-1 if axis == dim else 1 for axis in range(len(shape))])
    return factor_of


def centred(key, dims, width, limit, pieces=(), held_as=jnp.bfloat16):
    values = width * jax.random.normal(key, dims, jnp.float32)
    if pieces:
        values = values * level_of(key, dims, pieces, -0.22, 0.18)
    return jnp.clip(values, -limit, limit).astype(held_as)


def setup_inputs(seed: int = 0) -> dict:
    key_of = jax.random.split(jax.random.key(seed), 7)
    adjoint_now = centred(key_of[0], (GROUPS, 3, NX, NY, NZ), 1.0, 6.0, ((0, 2), (2, 16)), jnp.float32)
    adjoint_prev = centred(key_of[1], (GROUPS, 3, NX, NY, NZ), 1.0, 6.0, ((0, 2), (2, 16)), jnp.float32)
    forward_field = centred(key_of[2], (GROUPS, STEPS, 3, NX, NY, NZ), 1.0, 6.0, ((0, 2), (3, 16)), jnp.float32)
    density = jnp.clip(jnp.exp(math.log(2.0) - 1.3862944 * jax.random.uniform(key_of[3], (NX, NY, NZ), jnp.float32) ** level_of(key_of[3], (NX, NY, NZ), ((0, 16),), -0.2, 0.2)), 0.5, 2.0)
    lame_first = jnp.clip(jnp.exp(math.log(2.0) - 1.3862944 * jax.random.uniform(key_of[4], (NX, NY, NZ), jnp.float32) ** level_of(key_of[4], (NX, NY, NZ), ((0, 16),), -0.2, 0.2)), 0.5, 2.0)
    shear_modulus = jnp.clip(jnp.exp(math.log(1.2) - 1.3862944 * jax.random.uniform(key_of[5], (NX, NY, NZ), jnp.float32) ** level_of(key_of[5], (NX, NY, NZ), ((0, 16),), -0.2, 0.2)), 0.3, 1.2)
    return dict(adjoint_now=adjoint_now, adjoint_prev=adjoint_prev, forward_field=forward_field, density=density, lame_first=lame_first, shear_modulus=shear_modulus)


time_step = 0.3


def slope_long(values):
    return (values[2:] - values[:-2]) * 0.5


def slope_mid(values, axis):
    padded = jnp.pad(values, [(1, 1) if dimension == axis else (0, 0) for dimension in range(3)])
    upper = lax.slice_in_dim(padded, 2, padded.shape[axis], axis=axis)
    lower = lax.slice_in_dim(padded, 0, padded.shape[axis] - 2, axis=axis)
    return (upper - lower) * 0.5


def gradient(field):
    table = [[None, None, None], [None, None, None], [None, None, None]]
    for second in range(3):
        component = field[second]
        middle = component[1:-1]
        table[0][second] = slope_long(component)
        table[1][second] = slope_mid(middle, 1)
        table[2][second] = slope_mid(middle, 2)
    return table


def strain_of(table):
    strain = [[0.5 * (table[first][second] + table[second][first]) for second in range(3)] for first in range(3)]
    trace = strain[0][0] + strain[1][1] + strain[2][2]
    return strain, trace


def stress_of(strain, trace, first_lame, shear_part):
    stress = []
    for first in range(3):
        stress_row = []
        for second in range(3):
            entry = 2.0 * shear_part * strain[first][second]
            if first == second:
                entry = entry + first_lame * trace
            stress_row.append(entry)
        stress.append(stress_row)
    return stress


def divergence(stress):
    result = []
    for second in range(3):
        total = slope_long(stress[0][second])
        total = total + slope_mid(stress[1][second], 1)[1:-1]
        total = total + slope_mid(stress[2][second], 2)[1:-1]
        result.append(total)
    return result


def crop(values, count, axis):
    if count == 0:
        return values
    return lax.slice_in_dim(values, count, values.shape[axis] - count, axis=axis)


def kernel_terms(strain, trace, forward_strain, forward_trace, first_lame, shear_part):
    contracted = strain[0][0] * forward_strain[0][0]
    for first in range(3):
        for second in range(3):
            if first + second > 0:
                contracted = contracted + strain[first][second] * forward_strain[first][second]
    shear_term = -2.0 * time_step * shear_part * (contracted - trace * forward_trace / 3.0)
    bulk_term = -time_step * (first_lame + 2.0 * shear_part / 3.0) * trace * forward_trace
    return shear_term, bulk_term


def advance(wide, prev_cut, model_cut, dens_cut, forward_wide, slab_cells):
    strain, trace = strain_of(gradient(wide))
    stress = stress_of(strain, trace, model_cut[0], model_cut[1])
    accel = jnp.stack(divergence(stress))
    updated = 2.0 * crop(wide, 2, 1) - prev_cut + time_step * time_step * accel / dens_cut
    margin = (wide.shape[1] - slab_cells) // 2
    inner = [[crop(entry, margin - 1, 0) for entry in strain_row] for strain_row in strain]
    inner_trace = crop(trace, margin - 1, 0)
    forward_strain, forward_trace = strain_of(gradient(forward_wide))
    model_margin = (model_cut.shape[1] - slab_cells) // 2
    first_lame = crop(model_cut[0], model_margin, 0)
    shear_part = crop(model_cut[1], model_margin, 0)
    return updated, kernel_terms(inner, inner_trace, forward_strain, forward_trace, first_lame, shear_part)


def wrap(values, count, axis):
    size = values.shape[axis]
    head = lax.slice_in_dim(values, size - count, size, axis=axis)
    tail = lax.slice_in_dim(values, 0, count, axis=axis)
    return jnp.concatenate([head, values, tail], axis=axis)


def reference(adjoint_now, adjoint_prev, forward_field, density, lame_first, shear_modulus):
    moduli = jnp.stack([lame_first, shear_modulus])
    model_wide = wrap(moduli, 1, 1)
    shear_total = jnp.zeros(density.shape, jnp.float32)
    bulk_total = jnp.zeros(density.shape, jnp.float32)
    finals = []
    for group in range(GROUPS):
        current = adjoint_now[group]
        former = adjoint_prev[group]
        for step in range(STEPS):
            wide = wrap(current, 2, 1)
            forward_wide = wrap(forward_field[group, step], 1, 1)
            updated, terms = advance(wide, former, model_wide, density, forward_wide, NX)
            shear_total = shear_total + terms[0]
            bulk_total = bulk_total + terms[1]
            former = current
            current = updated
        finals.append(current)
    return jnp.stack(finals), shear_total, bulk_total
```

```python
import jax
import jax.numpy as jnp
from jax import lax
from jax.experimental import pallas as pl
from jax.experimental.pallas import tpu as pltpu
from jax.sharding import PartitionSpec as P

time_step = 0.3
step_squared = time_step * time_step


def difference_tools(rows, lanes):
    row = lax.broadcasted_iota(jnp.int32, (rows, lanes), 0)
    lane = lax.broadcasted_iota(jnp.int32, (rows, lanes), 1)

    def along_rows(values):
        upper = jnp.where(row == rows - 1, 0.0, pltpu.roll(values, rows - 1, 0))
        lower = jnp.where(row == 0, 0.0, pltpu.roll(values, 1, 0))
        return upper - lower

    def along_lanes(values):
        upper = jnp.where(lane == lanes - 1, 0.0, pltpu.roll(values, lanes - 1, 1))
        lower = jnp.where(lane == 0, 0.0, pltpu.roll(values, 1, 1))
        return upper - lower

    return along_rows, along_lanes


def strain_parts(before, middle, after, tools):
    along_rows, along_lanes = tools
    first = after[0] - before[0]
    second = along_rows(middle[1])
    third = along_lanes(middle[2])
    pair_12 = (after[1] - before[1]) + along_rows(middle[0])
    pair_13 = (after[2] - before[2]) + along_lanes(middle[0])
    pair_23 = along_rows(middle[2]) + along_lanes(middle[1])
    return (first, second, third, pair_12, pair_13, pair_23, first + second + third)


def normal_stress(parts, lame, shear):
    return (2.0 * shear * parts[0] + lame * parts[6], shear * parts[3], shear * parts[4])


def cross_force(parts, normal, lame, shear, tools):
    along_rows, along_lanes = tools
    pressure = lame * parts[6]
    twice = 2.0 * shear
    s_22 = twice * parts[1] + pressure
    s_33 = twice * parts[2] + pressure
    s_23 = shear * parts[5]
    return (
        along_rows(normal[1]) + along_lanes(normal[2]),
        along_rows(s_22) + along_lanes(s_23),
        along_rows(s_23) + along_lanes(s_33),
    )


def term_pair(parts, other, lame, shear):
    straight = parts[0] * other[0] + parts[1] * other[1] + parts[2] * other[2]
    mixed = parts[3] * other[3] + parts[4] * other[4] + parts[5] * other[5]
    traces = parts[6] * other[6]
    shear_term = shear * (
        (-0.5 * time_step) * straight - (0.25 * time_step) * mixed + (time_step / 6.0) * traces
    )
    bulk_term = (-0.25 * time_step) * (lame + (2.0 / 3.0) * shear) * traces
    return shear_term, bulk_term


def call(kernel, outs, args, in_spaces, out_spaces, scratch=(), vmem=40 << 20):
    shapes = [
        pltpu.VMEM(shape, jnp.float32) if space is pltpu.VMEM else jax.ShapeDtypeStruct(shape, jnp.float32)
        for shape, space in zip(outs, out_spaces)
    ]
    out_spaces = [space or pltpu.VMEM for space in out_spaces]
    return pl.pallas_call(
        kernel,
        out_shape=shapes,
        in_specs=[pl.BlockSpec(memory_space=space) for space in in_spaces],
        out_specs=[pl.BlockSpec(memory_space=space) for space in out_spaces],
        scratch_shapes=list(scratch),
        compiler_params=pltpu.CompilerParams(vmem_limit_bytes=vmem),
    )(*args)


def local(adjoint_now, adjoint_prev, forward_field, density, lame_first, shear_modulus):
    slabs = lax.axis_size("blk")
    events = lax.axis_size("event")
    cells, rows, lanes = density.shape
    steps = forward_field.shape[1]
    last = cells - 1
    band = rows // events
    plane = (rows, lanes)
    VM, SM, ANY = pltpu.VMEM, pltpu.SMEM, pl.ANY

    odd = lax.rem(lax.axis_index("blk"), 2)
    mine = lax.axis_index("event")
    place = jnp.stack([odd, mine]).astype(jnp.int32)
    near = [(i, i + 1 - 2 * (i % 2)) for i in range(slabs)]
    far = [(i, (i - 1 + 2 * (i % 2)) % slabs) for i in range(slabs)]
    others = [
        [(i, (i + shift) % events) for i in range(events)] for shift in range(1, events)
    ]

    now, prev, forward = adjoint_now[0], adjoint_prev[0], forward_field[0]

    def layer(place_ref, t):
        return t + place_ref[0] * (last - 2 * t)

    def sign(place_ref):
        return (1 - 2 * place_ref[0]).astype(jnp.float32)

    def pack(place_ref, now_ref, forward_ref, lame_ref, shear_ref, near_ref, far_ref, far_fwd_ref, sem):
        copies = []

        def face(t, step, out, fwd_out, fwd_base):
            for slot in range(2):
                copies.append((now_ref.at[:, layer(place_ref, t + slot * step)], out.at[pl.ds(3 * slot, 3)]))
            copies.append((lame_ref.at[layer(place_ref, t)], out.at[6]))
            copies.append((shear_ref.at[layer(place_ref, t)], out.at[7]))
            for k in range(steps):
                copies.append(
                    (forward_ref.at[k, :, layer(place_ref, t)], fwd_out.at[pl.ds(fwd_base + 3 * k, 3)])
                )

        face(0, 1, far_ref, far_fwd_ref, 0)
        face(last, -1, near_ref, near_ref, 8)
        started = [pltpu.make_async_copy(src, dst, sem.at[i]) for i, (src, dst) in enumerate(copies)]
        for copy in started:
            copy.start()
        for copy in started:
            copy.wait()

    near_out, far_out, far_fwd_out = call(
        pack,
        [(8 + 3 * steps, *plane), (8, *plane), (3 * steps, *plane)],
        (place, now, forward, lame_first, shear_modulus),
        [SM, ANY, ANY, ANY, ANY],
        [VM, VM, VM],
        [pltpu.SemaphoreType.DMA((8 + 2 * steps,))],
    )
    near_in = lax.ppermute(near_out, "blk", near)
    far_in = lax.ppermute(far_out, "blk", far)
    far_fwd_in = lax.ppermute(far_fwd_out, "blk", far)

    def first(
        place_ref, now_ref, prev_ref, forward_ref, dens_ref, lame_ref, shear_ref, near_ref,
        now_v, fwd_v, lame_v, shear_v, scale_v, next_v, near_next, terms_v,
        prev_v, dens_v, normal_v, sem,
    ):
        moves = [
            pltpu.make_async_copy(src, dst, sem.at[i])
            for i, (src, dst) in enumerate(
                [(now_ref, now_v), (lame_ref, lame_v), (shear_ref, shear_v), (forward_ref, fwd_v),
                 (prev_ref, prev_v), (dens_ref, dens_v)]
            )
        ]
        for move in moves:
            move.start()
        for move in moves:
            move.wait()
        sigma = sign(place_ref)
        tools = difference_tools(*plane)

        def at(t):
            return layer(place_ref, t)

        def field(t):
            if t <= last:
                return (now_v[0, at(t)] * sigma, now_v[1, at(t)], now_v[2, at(t)])
            base = 3 * (t - cells)
            return (near_ref[base] * sigma, near_ref[base + 1], near_ref[base + 2])

        def fwd(k, t):
            if t <= last:
                return (fwd_v[k, 0, at(t)] * sigma, fwd_v[k, 1, at(t)], fwd_v[k, 2, at(t)])
            base = 8 + 3 * k
            return (near_ref[base] * sigma, near_ref[base + 1], near_ref[base + 2])

        for t in range(cells):
            scale_v[t] = (0.25 * step_squared) / dens_v[at(t)]
        for t in range(1, cells + 1):
            parts = strain_parts(field(t - 1), field(t), field(t + 1), tools)
            if t <= last:
                lame, shear = lame_v[at(t)], shear_v[at(t)]
            else:
                lame, shear = near_ref[6], near_ref[7]
            normal = normal_stress(parts, lame, shear)
            for b in range(3):
                normal_v[b, t] = normal[b]
            if t <= last:
                force = cross_force(parts, normal, lame, shear, tools)
                for b in range(3):
                    next_v[b, t] = force[b]
                other = strain_parts(fwd(0, t - 1), fwd(0, t), fwd(0, t + 1), tools)
                pair = term_pair(parts, other, lame, shear)
                terms_v[0, t] = pair[0]
                terms_v[1, t] = pair[1]
        for t in range(cells):
            for b in range(3):
                force = normal_v[b, t + 1]
                if t > 0:
                    force = force + next_v[b, t]
                if t > 1:
                    force = force - normal_v[b, t - 1]
                old = prev_v[b, at(t)]
                if b == 0:
                    old = old * sigma
                new = 2.0 * field(t)[b] - old + scale_v[t] * force
                next_v[b, t] = new
                if t >= last - 1:
                    near_next[3 * (last - t) + b] = new

    now_v, fwd_v, lame_v, shear_v, scale_v, next_v, near_next, terms_v = call(
        first,
        [now.shape, forward.shape, density.shape, density.shape, density.shape, now.shape,
         (6, *plane), (2, cells, *plane)],
        (place, now, prev, forward, density, lame_first, shear_modulus, near_in),
        [SM] + [ANY] * 6 + [VM],
        [VM] * 8,
        [pltpu.VMEM(now.shape, jnp.float32), pltpu.VMEM(density.shape, jnp.float32),
         pltpu.VMEM((3, cells + 1, *plane), jnp.float32), pltpu.SemaphoreType.DMA((6,))],
    )
    near_next_in = lax.ppermute(near_next, "blk", near)

    def far_first(place_ref, now_v, lame_v, shear_v, scale_v, next_v, far_ref, far_next):
        sigma = sign(place_ref)
        tools = difference_tools(*plane)

        def at(t):
            return layer(place_ref, t)

        def field(t):
            if t >= 0:
                return (now_v[0, at(t)] * sigma, now_v[1, at(t)], now_v[2, at(t)])
            base = 3 * (-1 - t)
            return (far_ref[base] * sigma, far_ref[base + 1], far_ref[base + 2])

        outer = normal_stress(strain_parts(field(-2), field(-1), field(0), tools), far_ref[6], far_ref[7])
        lame, shear = lame_v[at(0)], shear_v[at(0)]
        parts = strain_parts(field(-1), field(0), field(1), tools)
        normal = normal_stress(parts, lame, shear)
        force = cross_force(parts, normal, lame, shear, tools)
        for b in range(3):
            far_next[b] = next_v[b, 0] + scale_v[0] * (force[b] - outer[b])
            far_next[3 + b] = next_v[b, 1] - scale_v[1] * normal[b]

    (far_next,) = call(
        far_first,
        [(6, *plane)],
        (place, now_v, lame_v, shear_v, scale_v, next_v, far_in),
        [SM] + [VM] * 6,
        [VM],
    )
    far_next_in = lax.ppermute(far_next, "blk", far)

    def second(
        place_ref, now_v, fwd_v, lame_v, shear_v, scale_v, next_v, terms_v, far_next_ref, near_next_ref,
        near_ref, far_ref, far_fwd_ref,
        final_v, keep_ref, send_ref, normal_v, total_v,
    ):
        sigma = sign(place_ref)
        tools = difference_tools(*plane)

        def at(t):
            return layer(place_ref, t)

        def start(t):
            if t >= 0:
                return (now_v[0, at(t)] * sigma, now_v[1, at(t)], now_v[2, at(t)])
            return (far_ref[0] * sigma, far_ref[1], far_ref[2])

        def field(t):
            if t < 2:
                return tuple(far_next_ref[3 * t + b] for b in range(3))
            if t <= last:
                return tuple(next_v[b, t] for b in range(3))
            base = 3 * (t - cells)
            return (-near_next_ref[base], near_next_ref[base + 1], near_next_ref[base + 2])

        def fwd(k, t):
            if t < 0:
                return (far_fwd_ref[3 * k] * sigma, far_fwd_ref[3 * k + 1], far_fwd_ref[3 * k + 2])
            if t <= last:
                return (fwd_v[k, 0, at(t)] * sigma, fwd_v[k, 1, at(t)], fwd_v[k, 2, at(t)])
            base = 8 + 3 * k
            return (near_ref[base] * sigma, near_ref[base + 1], near_ref[base + 2])

        for t in range(1, cells + 1):
            parts = strain_parts(field(t - 1), field(t), field(t + 1), tools)
            if t <= last:
                lame, shear = lame_v[at(t)], shear_v[at(t)]
            else:
                lame, shear = near_ref[6], near_ref[7]
            normal = normal_stress(parts, lame, shear)
            for b in range(3):
                normal_v[b, t] = normal[b]
            if t <= last:
                force = cross_force(parts, normal, lame, shear, tools)
                for b in range(3):
                    final_v[b, t] = force[b]
                other = strain_parts(fwd(1, t - 1), fwd(1, t), fwd(1, t + 1), tools)
                pair = term_pair(parts, other, lame, shear)
                for k in range(2):
                    total_v[k, t] = terms_v[k, t] + pair[k]
        for t in range(cells):
            for b in range(3):
                force = normal_v[b, t + 1]
                if t > 0:
                    force = force + final_v[b, t]
                if t > 1:
                    force = force - normal_v[b, t - 1]
                old = now_v[b, at(t)]
                if b == 0:
                    old = old * sigma
                final_v[b, t] = 2.0 * field(t)[b] - old + scale_v[t] * force
        parts = strain_parts(start(-1), start(0), start(1), tools)
        other = strain_parts(fwd(0, -1), fwd(0, 0), fwd(0, 1), tools)
        pair = term_pair(parts, other, lame_v[at(0)], shear_v[at(0)])
        for k in range(2):
            total_v[k, 0] = pair[k]
        own = place_ref[1]
        keep_ref[...] = total_v[:, :, pl.ds(pl.multiple_of(own * band, 8), band)]
        for shift in range(1, events):
            target = lax.rem(own + shift, events)
            send_ref[shift - 1] = total_v[:, :, pl.ds(pl.multiple_of(target * band, 8), band)]

    final_v, keep, send = call(
        second,
        [now.shape, (2, cells, band, lanes), (events - 1, 2, cells, band, lanes)],
        (place, now_v, fwd_v, lame_v, shear_v, scale_v, next_v, terms_v, far_next, near_next_in,
         near_in, far_in, far_fwd_in),
        [SM] + [VM] * 12,
        [VM] * 3,
        [pltpu.VMEM((3, cells + 1, *plane), jnp.float32), pltpu.VMEM((2, cells, *plane), jnp.float32)],
    )
    shared = [lax.ppermute(send[i], "event", others[i]) for i in range(events - 1)]

    def far_second(
        place_ref, now_v, fwd_v, lame_v, shear_v, scale_v, final_v, far_next_ref, next_v, far_ref, far_fwd_ref,
        far_next_in_ref,
        out_ref, keep_ref, send_ref, total_v,
    ):
        sigma = sign(place_ref)
        tools = difference_tools(*plane)

        def at(t):
            return layer(place_ref, t)

        def field(t):
            if t < 0:
                base = 3 * (-1 - t)
                return (-far_next_in_ref[base], far_next_in_ref[base + 1], far_next_in_ref[base + 2])
            return tuple(far_next_ref[3 * t + b] for b in range(3))

        def fwd(k, t):
            if t < 0:
                return (far_fwd_ref[3 * k] * sigma, far_fwd_ref[3 * k + 1], far_fwd_ref[3 * k + 2])
            return (fwd_v[k, 0, at(t)] * sigma, fwd_v[k, 1, at(t)], fwd_v[k, 2, at(t)])

        outer = normal_stress(strain_parts(field(-2), field(-1), field(0), tools), far_ref[6], far_ref[7])
        lame, shear = lame_v[at(0)], shear_v[at(0)]
        parts = strain_parts(field(-1), field(0), field(1), tools)
        normal = normal_stress(parts, lame, shear)
        force = cross_force(parts, normal, lame, shear, tools)
        other = strain_parts(fwd(1, -1), fwd(1, 0), fwd(1, 1), tools)
        pair = term_pair(parts, other, lame, shear)
        for k in range(2):
            total_v[k] = pair[k]
        own = place_ref[1]
        keep_ref[...] = total_v[:, pl.ds(pl.multiple_of(own * band, 8), band)]
        for shift in range(1, events):
            target = lax.rem(own + shift, events)
            send_ref[shift - 1] = total_v[:, pl.ds(pl.multiple_of(target * band, 8), band)]
        for t in range(cells):
            for b in range(3):
                value = final_v[b, t]
                if t == 0:
                    value = value + scale_v[0] * (force[b] - outer[b])
                if t == 1:
                    value = value - scale_v[1] * normal[b]
                if b == 0:
                    value = value * sigma
                out_ref[b, at(t)] = value

    result, far_keep, far_send = call(
        far_second,
        [now.shape, (2, band, lanes), (events - 1, 2, band, lanes)],
        (place, now_v, fwd_v, lame_v, shear_v, scale_v, final_v, far_next, next_v, far_in, far_fwd_in,
         far_next_in),
        [SM] + [VM] * 11,
        [None, VM, VM],
        [pltpu.VMEM((2, *plane), jnp.float32)],
    )
    far_shared = [lax.ppermute(far_send[i], "event", others[i]) for i in range(events - 1)]

    def finish(place_ref, keep_ref, far_keep_ref, *rest):
        parts = rest[: 2 * (events - 1)]
        outs = rest[2 * (events - 1) :]
        for k in range(2):
            for t in range(cells):
                value = keep_ref[k, t]
                for i in range(events - 1):
                    value = value + parts[i][k, t]
                if t == 0:
                    value = value + far_keep_ref[k]
                    for i in range(events - 1):
                        value = value + parts[events - 1 + i][k]
                outs[k][layer(place_ref, t)] = value

    band_shear, band_bulk = call(
        finish,
        [(cells, band, lanes)] * 2,
        (place, keep, far_keep, *shared, *far_shared),
        [SM] + [VM] * (2 + 2 * (events - 1)),
        [None] * 2,
    )
    return (result[None], band_shear, band_bulk)


def solution(mesh):
    in_specs = (
        P("event", None, "blk", None, None),
        P("event", None, "blk", None, None),
        P("event", None, None, "blk", None, None),
        P("blk", None, None),
        P("blk", None, None),
        P("blk", None, None),
    )
    out_specs = (
        P("event", None, "blk", None, None),
        P("blk", "event", None),
        P("blk", "event", None),
    )
    return jax.shard_map(local, mesh=mesh, in_specs=in_specs, out_specs=out_specs, check_vma=False)
```

```python
import jax
import jax.numpy as jnp
from jax import lax
from jax.experimental import pallas as pl
from jax.experimental.pallas import tpu as pltpu
from jax.sharding import PartitionSpec as P

time_step = 0.3
step_squared = time_step * time_step


def difference_tools(rows, lanes):
    row = lax.broadcasted_iota(jnp.int32, (rows, lanes), 0)
    lane = lax.broadcasted_iota(jnp.int32, (rows, lanes), 1)

    def along_rows(values):
        upper = jnp.where(row == rows - 1, 0.0, pltpu.roll(values, rows - 1, 0))
        lower = jnp.where(row == 0, 0.0, pltpu.roll(values, 1, 0))
        return upper - lower

    def along_lanes(values):
        upper = jnp.where(lane == lanes - 1, 0.0, pltpu.roll(values, lanes - 1, 1))
        lower = jnp.where(lane == 0, 0.0, pltpu.roll(values, 1, 1))
        return upper - lower

    return along_rows, along_lanes


def strain_parts(before, middle, after, tools):
    along_rows, along_lanes = tools
    first = after[0] - before[0]
    second = along_rows(middle[1])
    third = along_lanes(middle[2])
    pair_12 = (after[1] - before[1]) + along_rows(middle[0])
    pair_13 = (after[2] - before[2]) + along_lanes(middle[0])
    pair_23 = along_rows(middle[2]) + along_lanes(middle[1])
    return (first, second, third, pair_12, pair_13, pair_23, first + second + third)


def normal_stress(parts, lame, shear):
    return (2.0 * shear * parts[0] + lame * parts[6], shear * parts[3], shear * parts[4])


def cross_force(parts, normal, lame, shear, tools):
    along_rows, along_lanes = tools
    pressure = lame * parts[6]
    twice = 2.0 * shear
    s_22 = twice * parts[1] + pressure
    s_33 = twice * parts[2] + pressure
    s_23 = shear * parts[5]
    return (
        along_rows(normal[1]) + along_lanes(normal[2]),
        along_rows(s_22) + along_lanes(s_23),
        along_rows(s_23) + along_lanes(s_33),
    )


def term_pair(parts, other, lame, shear):
    straight = parts[0] * other[0] + parts[1] * other[1] + parts[2] * other[2]
    mixed = parts[3] * other[3] + parts[4] * other[4] + parts[5] * other[5]
    traces = parts[6] * other[6]
    shear_term = shear * (
        (-0.5 * time_step) * straight - (0.25 * time_step) * mixed + (time_step / 6.0) * traces
    )
    bulk_term = (-0.25 * time_step) * (lame + (2.0 / 3.0) * shear) * traces
    return shear_term, bulk_term


def call(kernel, outs, args, in_spaces, out_spaces, scratch=(), vmem=40 << 20):
    shapes = [
        pltpu.VMEM(shape, jnp.float32) if space is pltpu.VMEM else jax.ShapeDtypeStruct(shape, jnp.float32)
        for shape, space in zip(outs, out_spaces)
    ]
    out_spaces = [space or pltpu.VMEM for space in out_spaces]
    return pl.pallas_call(
        kernel,
        out_shape=shapes,
        in_specs=[pl.BlockSpec(memory_space=space) for space in in_spaces],
        out_specs=[pl.BlockSpec(memory_space=space) for space in out_spaces],
        scratch_shapes=list(scratch),
        compiler_params=pltpu.CompilerParams(vmem_limit_bytes=vmem),
    )(*args)


def local(adjoint_now, adjoint_prev, forward_field, density, lame_first, shear_modulus):
    slabs = lax.axis_size("blk")
    events = lax.axis_size("event")
    cells, rows, lanes = density.shape
    steps = forward_field.shape[1]
    last = cells - 1
    band = rows // events
    plane = (rows, lanes)
    VM, SM, ANY = pltpu.VMEM, pltpu.SMEM, pl.ANY

    odd = lax.rem(lax.axis_index("blk"), 2)
    mine = lax.axis_index("event")
    place = jnp.stack([odd, mine]).astype(jnp.int32)
    near = [(i, i + 1 - 2 * (i % 2)) for i in range(slabs)]
    far = [(i, (i - 1 + 2 * (i % 2)) % slabs) for i in range(slabs)]
    others = [
        [(i, (i + shift) % events) for i in range(events)] for shift in range(1, events)
    ]

    in_hbm = [
        pltpu.with_memory_space_constraint(x, pltpu.HBM)
        for x in (adjoint_now[0], adjoint_prev[0], forward_field[0], density, lame_first, shear_modulus)
    ]
    now, prev, forward, density, lame_first, shear_modulus = in_hbm

    def layer(place_ref, t):
        return t + place_ref[0] * (last - 2 * t)

    def sign(place_ref):
        return (1 - 2 * place_ref[0]).astype(jnp.float32)

    def pack(place_ref, now_ref, forward_ref, lame_ref, shear_ref, near_ref, far_ref, far_fwd_ref, sem):
        copies = []

        def face(t, step, out, fwd_out, fwd_base):
            for slot in range(2):
                copies.append((now_ref.at[:, layer(place_ref, t + slot * step)], out.at[pl.ds(3 * slot, 3)]))
            copies.append((lame_ref.at[layer(place_ref, t)], out.at[6]))
            copies.append((shear_ref.at[layer(place_ref, t)], out.at[7]))
            for k in range(steps):
                copies.append(
                    (forward_ref.at[k, :, layer(place_ref, t)], fwd_out.at[pl.ds(fwd_base + 3 * k, 3)])
                )

        face(0, 1, far_ref, far_fwd_ref, 0)
        face(last, -1, near_ref, near_ref, 8)
        started = [pltpu.make_async_copy(src, dst, sem.at[i]) for i, (src, dst) in enumerate(copies)]
        for copy in started:
            copy.start()
        for copy in started:
            copy.wait()

    near_out, far_out, far_fwd_out = call(
        pack,
        [(8 + 3 * steps, *plane), (8, *plane), (3 * steps, *plane)],
        (place, now, forward, lame_first, shear_modulus),
        [SM, ANY, ANY, ANY, ANY],
        [VM, VM, VM],
        [pltpu.SemaphoreType.DMA((8 + 2 * steps,))],
    )
    near_in = lax.ppermute(near_out, "blk", near)
    far_in = lax.ppermute(far_out, "blk", far)
    far_fwd_in = lax.ppermute(far_fwd_out, "blk", far)

    def split(place_ref, terms_ref, layers, keep_ref, send_ref):
        own = place_ref[1]
        for shift in range(events):
            target = lax.rem(own + shift, events) if shift else own
            start = pl.multiple_of(target * band, 8)
            out = send_ref.at[shift - 1] if shift else keep_ref
            for k in range(2):
                for i, t in enumerate(layers):
                    out[k, i] = terms_ref[k, t, pl.ds(start, band)]

    def first(
        place_ref, now_ref, prev_ref, forward_ref, dens_ref, lame_ref, shear_ref, near_ref,
        now_v, fwd_v, lame_v, shear_v, scale_v, next_v, near_next, terms_v, keep_ref, send_ref,
        prev_v, dens_v, normal_v, sem,
    ):
        moves = [
            pltpu.make_async_copy(src, dst, sem.at[i])
            for i, (src, dst) in enumerate(
                [(now_ref, now_v), (lame_ref, lame_v), (shear_ref, shear_v), (forward_ref, fwd_v),
                 (prev_ref, prev_v), (dens_ref, dens_v)]
            )
        ]
        for move in moves:
            move.start()
        for move in moves:
            move.wait()
        sigma = sign(place_ref)
        tools = difference_tools(*plane)

        def at(t):
            return layer(place_ref, t)

        def field(t):
            if t <= last:
                return (now_v[0, at(t)] * sigma, now_v[1, at(t)], now_v[2, at(t)])
            base = 3 * (t - cells)
            return (near_ref[base] * sigma, near_ref[base + 1], near_ref[base + 2])

        def fwd(k, t):
            if t <= last:
                return (fwd_v[k, 0, at(t)] * sigma, fwd_v[k, 1, at(t)], fwd_v[k, 2, at(t)])
            base = 8 + 3 * k
            return (near_ref[base] * sigma, near_ref[base + 1], near_ref[base + 2])

        for t in range(cells):
            scale_v[t] = (0.25 * step_squared) / dens_v[at(t)]
        for t in range(1, cells + 1):
            parts = strain_parts(field(t - 1), field(t), field(t + 1), tools)
            if t <= last:
                lame, shear = lame_v[at(t)], shear_v[at(t)]
            else:
                lame, shear = near_ref[6], near_ref[7]
            normal = normal_stress(parts, lame, shear)
            for b in range(3):
                normal_v[b, t] = normal[b]
            if t <= last:
                force = cross_force(parts, normal, lame, shear, tools)
                for b in range(3):
                    next_v[b, t] = force[b]
                other = strain_parts(fwd(0, t - 1), fwd(0, t), fwd(0, t + 1), tools)
                pair = term_pair(parts, other, lame, shear)
                terms_v[0, t] = pair[0]
                terms_v[1, t] = pair[1]
        for t in range(cells):
            for b in range(3):
                force = normal_v[b, t + 1]
                if t > 0:
                    force = force + next_v[b, t]
                if t > 1:
                    force = force - normal_v[b, t - 1]
                old = prev_v[b, at(t)]
                if b == 0:
                    old = old * sigma
                new = 2.0 * field(t)[b] - old + scale_v[t] * force
                next_v[b, t] = new
                if t >= last - 1:
                    near_next[3 * (last - t) + b] = new
        for t in early:
            lame, shear = lame_v[at(t)], shear_v[at(t)]
            fields = [tuple(next_v[b, t + d] for b in range(3)) for d in (-1, 0, 1)]
            parts = strain_parts(*fields, tools)
            other = strain_parts(fwd(1, t - 1), fwd(1, t), fwd(1, t + 1), tools)
            pair = term_pair(parts, other, lame, shear)
            for k in range(2):
                terms_v[k, t] = terms_v[k, t] + pair[k]
        split(place_ref, terms_v, early, keep_ref, send_ref)

    early = list(range(3, last))
    middle = [1, 2, last]
    now_v, fwd_v, lame_v, shear_v, scale_v, next_v, near_next, terms_v, keep, send = call(
        first,
        [now.shape, forward.shape, density.shape, density.shape, density.shape, now.shape,
         (6, *plane), (2, cells, *plane), (2, len(early), band, lanes), (events - 1, 2, len(early), band, lanes)],
        (place, now, prev, forward, density, lame_first, shear_modulus, near_in),
        [SM] + [ANY] * 6 + [VM],
        [VM] * 10,
        [pltpu.VMEM(now.shape, jnp.float32), pltpu.VMEM(density.shape, jnp.float32),
         pltpu.VMEM((3, cells + 1, *plane), jnp.float32), pltpu.SemaphoreType.DMA((6,))],
    )
    near_next_in = lax.ppermute(near_next, "blk", near)
    shared = [lax.ppermute(send[i], "event", others[i]) for i in range(events - 1)]

    def far_first(place_ref, now_v, lame_v, shear_v, scale_v, next_v, far_ref, far_next):
        sigma = sign(place_ref)
        tools = difference_tools(*plane)

        def at(t):
            return layer(place_ref, t)

        def field(t):
            if t >= 0:
                return (now_v[0, at(t)] * sigma, now_v[1, at(t)], now_v[2, at(t)])
            base = 3 * (-1 - t)
            return (far_ref[base] * sigma, far_ref[base + 1], far_ref[base + 2])

        outer = normal_stress(strain_parts(field(-2), field(-1), field(0), tools), far_ref[6], far_ref[7])
        lame, shear = lame_v[at(0)], shear_v[at(0)]
        parts = strain_parts(field(-1), field(0), field(1), tools)
        normal = normal_stress(parts, lame, shear)
        force = cross_force(parts, normal, lame, shear, tools)
        for b in range(3):
            far_next[b] = next_v[b, 0] + scale_v[0] * (force[b] - outer[b])
            far_next[3 + b] = next_v[b, 1] - scale_v[1] * normal[b]

    (far_next,) = call(
        far_first,
        [(6, *plane)],
        (place, now_v, lame_v, shear_v, scale_v, next_v, far_in),
        [SM] + [VM] * 6,
        [VM],
    )
    far_next_in = lax.ppermute(far_next, "blk", far)

    def second(
        place_ref, now_v, fwd_v, lame_v, shear_v, scale_v, next_v, terms_v, far_next_ref, near_next_ref,
        near_ref, far_ref, far_fwd_ref,
        final_v, total_v, slope_v, keep_ref, send_ref, normal_v,
    ):
        sigma = sign(place_ref)
        tools = difference_tools(*plane)

        def at(t):
            return layer(place_ref, t)

        def start(t):
            if t >= 0:
                return (now_v[0, at(t)] * sigma, now_v[1, at(t)], now_v[2, at(t)])
            return (far_ref[0] * sigma, far_ref[1], far_ref[2])

        def field(t):
            if t < 2:
                return tuple(far_next_ref[3 * t + b] for b in range(3))
            if t <= last:
                return tuple(next_v[b, t] for b in range(3))
            base = 3 * (t - cells)
            return (-near_next_ref[base], near_next_ref[base + 1], near_next_ref[base + 2])

        def fwd(k, t):
            if t < 0:
                return (far_fwd_ref[3 * k] * sigma, far_fwd_ref[3 * k + 1], far_fwd_ref[3 * k + 2])
            if t <= last:
                return (fwd_v[k, 0, at(t)] * sigma, fwd_v[k, 1, at(t)], fwd_v[k, 2, at(t)])
            base = 8 + 3 * k
            return (near_ref[base] * sigma, near_ref[base + 1], near_ref[base + 2])

        for t in range(1, cells + 1):
            parts = strain_parts(field(t - 1), field(t), field(t + 1), tools)
            if t <= last:
                lame, shear = lame_v[at(t)], shear_v[at(t)]
            else:
                lame, shear = near_ref[6], near_ref[7]
            normal = normal_stress(parts, lame, shear)
            for b in range(3):
                normal_v[b, t] = normal[b]
            if t <= last:
                force = cross_force(parts, normal, lame, shear, tools)
                for b in range(3):
                    final_v[b, t] = force[b]
                if t in middle:
                    other = strain_parts(fwd(1, t - 1), fwd(1, t), fwd(1, t + 1), tools)
                    pair = term_pair(parts, other, lame, shear)
                    for k in range(2):
                        total_v[k, t] = terms_v[k, t] + pair[k]
        for t in range(cells):
            for b in range(3):
                force = normal_v[b, t + 1]
                if t > 0:
                    force = force + final_v[b, t]
                if t > 1:
                    force = force - normal_v[b, t - 1]
                old = now_v[b, at(t)]
                if b == 0:
                    old = old * sigma
                final_v[b, t] = 2.0 * field(t)[b] - old + scale_v[t] * force
        split(place_ref, total_v, middle, keep_ref, send_ref)
        parts = strain_parts(start(-1), start(0), start(1), tools)
        other = strain_parts(fwd(0, -1), fwd(0, 0), fwd(0, 1), tools)
        lame, shear = lame_v[at(0)], shear_v[at(0)]
        pair = term_pair(parts, other, lame, shear)
        empty = jnp.zeros(plane, jnp.float32)
        parts = strain_parts((empty, empty, empty), field(0), field(1), tools)
        other = strain_parts(fwd(1, -1), fwd(1, 0), fwd(1, 1), tools)
        rest = term_pair(parts, other, lame, shear)
        for k in range(2):
            total_v[k, 0] = pair[k] + rest[k]
        slope_v[0] = shear * ((0.5 * time_step) * other[0] - (time_step / 6.0) * other[6])
        slope_v[1] = (0.25 * time_step) * shear * other[3]
        slope_v[2] = (0.25 * time_step) * shear * other[4]
        slope_v[3] = (0.25 * time_step) * (lame + (2.0 / 3.0) * shear) * other[6]

    final_v, total_v, slope_v, keep_mid, send_mid = call(
        second,
        [now.shape, (2, cells, *plane), (4, *plane),
         (2, len(middle), band, lanes), (events - 1, 2, len(middle), band, lanes)],
        (place, now_v, fwd_v, lame_v, shear_v, scale_v, next_v, terms_v, far_next, near_next_in,
         near_in, far_in, far_fwd_in),
        [SM] + [VM] * 12,
        [VM] * 5,
        [pltpu.VMEM((3, cells + 1, *plane), jnp.float32)],
    )
    shared_mid = [lax.ppermute(send_mid[i], "event", others[i]) for i in range(events - 1)]

    def far_terms(place_ref, total_ref, slope_ref, far_next_in_ref, keep_ref, send_ref, total_v):
        outer = (-far_next_in_ref[0], far_next_in_ref[1], far_next_in_ref[2])
        shear_part = total_ref[0, 0]
        for b in range(3):
            shear_part = shear_part + slope_ref[b] * outer[b]
        total_v[0, 0] = shear_part
        total_v[1, 0] = total_ref[1, 0] + slope_ref[3] * outer[0]
        split(place_ref, total_v, [0], keep_ref, send_ref)

    far_keep, far_send = call(
        far_terms,
        [(2, 1, band, lanes), (events - 1, 2, 1, band, lanes)],
        (place, total_v, slope_v, far_next_in),
        [SM] + [VM] * 3,
        [VM] * 2,
        [pltpu.VMEM((2, 1, *plane), jnp.float32)],
    )
    far_shared = [lax.ppermute(far_send[i], "event", others[i]) for i in range(events - 1)]

    def far_second(
        place_ref, lame_v, shear_v, scale_v, final_v, far_next_ref, next_v, far_ref, far_next_in_ref, out_ref
    ):
        sigma = sign(place_ref)
        tools = difference_tools(*plane)

        def at(t):
            return layer(place_ref, t)

        def field(t):
            if t < 0:
                base = 3 * (-1 - t)
                return (-far_next_in_ref[base], far_next_in_ref[base + 1], far_next_in_ref[base + 2])
            return tuple(far_next_ref[3 * t + b] for b in range(3))

        outer = normal_stress(strain_parts(field(-2), field(-1), field(0), tools), far_ref[6], far_ref[7])
        lame, shear = lame_v[at(0)], shear_v[at(0)]
        parts = strain_parts(field(-1), field(0), field(1), tools)
        normal = normal_stress(parts, lame, shear)
        force = cross_force(parts, normal, lame, shear, tools)
        for t in range(cells):
            for b in range(3):
                value = final_v[b, t]
                if t == 0:
                    value = value + scale_v[0] * (force[b] - outer[b])
                if t == 1:
                    value = value - scale_v[1] * normal[b]
                if b == 0:
                    value = value * sigma
                out_ref[b, at(t)] = value

    (result,) = call(
        far_second,
        [now.shape],
        (place, lame_v, shear_v, scale_v, final_v, far_next, next_v, far_in, far_next_in),
        [SM] + [VM] * 8,
        [None],
    )

    def finish(place_ref, *rest):
        width = events
        outs = rest[3 * width :]
        for group, layers in enumerate((early, middle, [0])):
            parts = rest[group * width : (group + 1) * width]
            for k in range(2):
                for i, t in enumerate(layers):
                    value = parts[0][k, i]
                    for part in parts[1:]:
                        value = value + part[k, i]
                    outs[k][layer(place_ref, t)] = value

    band_shear, band_bulk = call(
        finish,
        [(cells, band, lanes)] * 2,
        (place, keep, *shared, keep_mid, *shared_mid, far_keep, *far_shared),
        [SM] + [VM] * (3 * events),
        [None] * 2,
    )
    return (result[None], band_shear, band_bulk)


def solution(mesh):
    in_specs = (
        P("event", None, "blk", None, None),
        P("event", None, "blk", None, None),
        P("event", None, None, "blk", None, None),
        P("blk", None, None),
        P("blk", None, None),
        P("blk", None, None),
    )
    out_specs = (
        P("event", None, "blk", None, None),
        P("blk", "event", None),
        P("blk", "event", None),
    )
    return jax.shard_map(local, mesh=mesh, in_specs=in_specs, out_specs=out_specs, check_vma=False)
```

```python
import jax
import jax.numpy as jnp
from jax import lax
from jax.experimental import pallas as pl
from jax.experimental.pallas import tpu as pltpu
from jax.sharding import PartitionSpec as P

time_step = 0.3
step_squared = time_step * time_step


def difference_tools(rows, lanes):
    row = lax.broadcasted_iota(jnp.int32, (rows, lanes), 0)
    lane = lax.broadcasted_iota(jnp.int32, (rows, lanes), 1)

    def along_rows(values):
        upper = jnp.where(row == rows - 1, 0.0, pltpu.roll(values, rows - 1, 0))
        lower = jnp.where(row == 0, 0.0, pltpu.roll(values, 1, 0))
        return upper - lower

    def along_lanes(values):
        upper = jnp.where(lane == lanes - 1, 0.0, pltpu.roll(values, lanes - 1, 1))
        lower = jnp.where(lane == 0, 0.0, pltpu.roll(values, 1, 1))
        return upper - lower

    key = lax.broadcasted_iota(jnp.int32, (3 * lanes, lanes), 0) % lanes
    out = lax.broadcasted_iota(jnp.int32, (3 * lanes, lanes), 1)
    weights = ((key == out + 1).astype(jnp.float32) - (key == out - 1).astype(jnp.float32)).astype(jnp.bfloat16)

    def along_lanes_three(fields):
        values = jnp.concatenate(fields, axis=0)
        high = values.astype(jnp.bfloat16)
        rest = values - high.astype(jnp.float32)
        middle = rest.astype(jnp.bfloat16)
        low = (rest - middle.astype(jnp.float32)).astype(jnp.bfloat16)
        parts = jnp.concatenate([high, middle, low], axis=1)
        result = jnp.dot(parts, weights, preferred_element_type=jnp.float32)
        return [result[rows * b : rows * (b + 1)] for b in range(len(fields))]

    return along_rows, along_lanes, along_lanes_three


def strain_parts(before, middle, after, tools):
    along_rows, along_lanes, along_lanes_three = tools
    first = after[0] - before[0]
    second = along_rows(middle[1])
    third = along_lanes(middle[2])
    pair_12 = (after[1] - before[1]) + along_rows(middle[0])
    pair_13 = (after[2] - before[2]) + along_lanes(middle[0])
    pair_23 = along_rows(middle[2]) + along_lanes(middle[1])
    return (first, second, third, pair_12, pair_13, pair_23, first + second + third)


def normal_stress(parts, lame, shear):
    return (2.0 * shear * parts[0] + lame * parts[6], shear * parts[3], shear * parts[4])


def cross_force(parts, normal, lame, shear, tools):
    along_rows, along_lanes, along_lanes_three = tools
    pressure = lame * parts[6]
    twice = 2.0 * shear
    s_22 = twice * parts[1] + pressure
    s_33 = twice * parts[2] + pressure
    s_23 = shear * parts[5]
    third_of = along_lanes_three((normal[2], s_23, s_33))
    return (
        along_rows(normal[1]) + third_of[0],
        along_rows(s_22) + third_of[1],
        along_rows(s_23) + third_of[2],
    )


def term_pair(parts, other, lame, shear):
    straight = parts[0] * other[0] + parts[1] * other[1] + parts[2] * other[2]
    mixed = parts[3] * other[3] + parts[4] * other[4] + parts[5] * other[5]
    traces = parts[6] * other[6]
    shear_term = shear * (
        (-0.5 * time_step) * straight - (0.25 * time_step) * mixed + (time_step / 6.0) * traces
    )
    bulk_term = (-0.25 * time_step) * (lame + (2.0 / 3.0) * shear) * traces
    return shear_term, bulk_term


def call(kernel, outs, args, in_spaces, out_spaces, scratch=(), vmem=40 << 20):
    shapes = [
        pltpu.VMEM(shape, jnp.float32) if space is pltpu.VMEM else jax.ShapeDtypeStruct(shape, jnp.float32)
        for shape, space in zip(outs, out_spaces)
    ]
    out_spaces = [space or pltpu.VMEM for space in out_spaces]
    return pl.pallas_call(
        kernel,
        out_shape=shapes,
        in_specs=[pl.BlockSpec(memory_space=space) for space in in_spaces],
        out_specs=[pl.BlockSpec(memory_space=space) for space in out_spaces],
        scratch_shapes=list(scratch),
        compiler_params=pltpu.CompilerParams(vmem_limit_bytes=vmem),
    )(*args)


def local(adjoint_now, adjoint_prev, forward_field, density, lame_first, shear_modulus):
    slabs = lax.axis_size("blk")
    events = lax.axis_size("event")
    cells, rows, lanes = density.shape
    steps = forward_field.shape[1]
    last = cells - 1
    band = rows // events
    plane = (rows, lanes)
    VM, SM, ANY = pltpu.VMEM, pltpu.SMEM, pl.ANY

    near = [(i, i + 1 - 2 * (i % 2)) for i in range(slabs)]
    far = [(i, (i - 1 + 2 * (i % 2)) % slabs) for i in range(slabs)]
    others = [
        [(i, (i + shift) % events) for i in range(events)] for shift in range(1, events)
    ]

    in_hbm = [
        pltpu.with_memory_space_constraint(x, pltpu.HBM)
        for x in (adjoint_now[0], adjoint_prev[0], forward_field[0], density, lame_first, shear_modulus)
    ]
    now_hbm, prev, forward_hbm, density, lame_hbm, shear_hbm = in_hbm
    now, forward = adjoint_now[0], forward_field[0]

    def where():
        return lax.rem(lax.axis_index("blk"), 2), lax.axis_index("event")

    def layer(place_ref, t):
        return t + place_ref[0] * (last - 2 * t)

    def far_slot(place_ref, n):
        return (1 - n) + place_ref[0] * (2 * n - 1)

    def near_slot(place_ref, n):
        return n + place_ref[0] * (1 - 2 * n)

    def sign(place_ref):
        return (1 - 2 * place_ref[0]).astype(jnp.float32)

    def pack(now_ref, forward_ref, lame_ref, shear_ref, near_ref, far_ref, far_fwd_ref, sem):
        place_ref = where()
        odd = place_ref[0]
        faces = ((far_ref, layer(place_ref, 0), odd * (cells - 2)), (near_ref, layer(place_ref, last), (1 - odd) * (cells - 2)))
        copies = []
        for out, at, low in faces:
            copies.append((now_ref.at[:, pl.ds(low, 2)], out.at[pl.ds(0, 3)]))
            copies.append((lame_ref.at[at], out.at[3, 0]))
            copies.append((shear_ref.at[at], out.at[3, 1]))
        copies.append((forward_ref.at[:, :, layer(place_ref, 0)], far_fwd_ref))
        for k in range(steps):
            copies.append((forward_ref.at[k, :, layer(place_ref, last)], near_ref.at[pl.ds(4, 3), k]))
        started = [pltpu.make_async_copy(src, dst, sem.at[i]) for i, (src, dst) in enumerate(copies)]
        for copy in started:
            copy.start()
        for copy in started:
            copy.wait()

    near_out, far_out, far_fwd_out = call(
        pack,
        [(7, 2, *plane), (4, 2, *plane), (steps, 3, *plane)],
        (now_hbm, forward_hbm, lame_hbm, shear_hbm),
        [ANY, ANY, ANY, ANY],
        [VM, VM, VM],
        [pltpu.SemaphoreType.DMA((7 + steps,))],
    )
    near_in = lax.ppermute(near_out, "blk", near)
    far_in = lax.ppermute(far_out, "blk", far)
    far_fwd_in = lax.ppermute(far_fwd_out, "blk", far)

    def split(place_ref, terms_ref, layers, keep_ref, send_ref):
        own = place_ref[1]
        for shift in range(events):
            target = lax.rem(own + shift, events) if shift else own
            start = pl.multiple_of(target * band, 8)
            out = send_ref.at[shift - 1] if shift else keep_ref
            for k in range(2):
                for i, t in enumerate(layers):
                    out[k, i] = terms_ref[k, t, pl.ds(start, band)]

    def first(now_v, prev_ref, fwd_v, dens_ref, lame_v, shear_v, near_ref,
        scale_v, next_v, near_next, terms_v, keep_ref, send_ref,
        prev_v, dens_v, normal_v, sem,
    ):
        place_ref = where()
        moves = [
            pltpu.make_async_copy(src, dst, sem.at[i])
            for i, (src, dst) in enumerate(
                [(dens_ref, dens_v), (prev_ref, prev_v)]
            )
        ]
        for move in moves:
            move.start()
        sigma = sign(place_ref)
        tools = difference_tools(*plane)

        def at(t):
            return layer(place_ref, t)

        def field(t):
            if t <= last:
                return (now_v[0, at(t)] * sigma, now_v[1, at(t)], now_v[2, at(t)])
            slot = near_slot(place_ref, t - cells)
            return (near_ref[0, slot] * sigma, near_ref[1, slot], near_ref[2, slot])

        def fwd(k, t):
            if t <= last:
                return (fwd_v[k, 0, at(t)] * sigma, fwd_v[k, 1, at(t)], fwd_v[k, 2, at(t)])
            return (near_ref[4, k] * sigma, near_ref[5, k], near_ref[6, k])

        for t in range(1, cells + 1):
            parts = strain_parts(field(t - 1), field(t), field(t + 1), tools)
            if t <= last:
                lame, shear = lame_v[at(t)], shear_v[at(t)]
            else:
                lame, shear = near_ref[3, 0], near_ref[3, 1]
            normal = normal_stress(parts, lame, shear)
            for b in range(3):
                normal_v[b, t] = normal[b]
            if t <= last:
                force = cross_force(parts, normal, lame, shear, tools)
                for b in range(3):
                    next_v[b, t] = force[b]
                other = strain_parts(fwd(0, t - 1), fwd(0, t), fwd(0, t + 1), tools)
                pair = term_pair(parts, other, lame, shear)
                terms_v[0, t] = pair[0]
                terms_v[1, t] = pair[1]
        for move in moves:
            move.wait()
        for t in range(cells):
            scale_v[t] = (0.25 * step_squared) / dens_v[at(t)]
        for t in range(cells):
            for b in range(3):
                force = normal_v[b, t + 1]
                if t > 0:
                    force = force + next_v[b, t]
                if t > 1:
                    force = force - normal_v[b, t - 1]
                old = prev_v[b, at(t)]
                if b == 0:
                    old = old * sigma
                new = 2.0 * field(t)[b] - old + scale_v[t] * force
                next_v[b, t] = new
                if t >= last - 1:
                    near_next[3 * (last - t) + b] = new
        for t in early:
            lame, shear = lame_v[at(t)], shear_v[at(t)]
            fields = [tuple(next_v[b, t + d] for b in range(3)) for d in (-1, 0, 1)]
            parts = strain_parts(*fields, tools)
            other = strain_parts(fwd(1, t - 1), fwd(1, t), fwd(1, t + 1), tools)
            pair = term_pair(parts, other, lame, shear)
            for k in range(2):
                terms_v[k, t] = terms_v[k, t] + pair[k]
        split(place_ref, terms_v, early, keep_ref, send_ref)

    early = list(range(3, last))
    middle = [1, 2, last]
    now_v, fwd_v, lame_v, shear_v = now, forward, lame_first, shear_modulus
    scale_v, next_v, near_next, terms_v, keep, send = call(
        first,
        [density.shape, now.shape,
         (6, *plane), (2, cells, *plane), (2, len(early), band, lanes), (events - 1, 2, len(early), band, lanes)],
        (now, prev, forward, density, lame_first, shear_modulus, near_in),
        [VM, ANY, VM, ANY, VM, VM, VM],
        [VM] * 6,
        [pltpu.VMEM(now.shape, jnp.float32), pltpu.VMEM(density.shape, jnp.float32),
         pltpu.VMEM((3, cells + 1, *plane), jnp.float32), pltpu.SemaphoreType.DMA((2,))],
    )
    near_next_in = lax.ppermute(near_next, "blk", near)
    shared = [lax.ppermute(send[i], "event", others[i]) for i in range(events - 1)]

    def far_first(now_v, lame_v, shear_v, scale_v, next_v, far_ref, far_next):
        place_ref = where()
        sigma = sign(place_ref)
        tools = difference_tools(*plane)

        def at(t):
            return layer(place_ref, t)

        def field(t):
            if t >= 0:
                return (now_v[0, at(t)] * sigma, now_v[1, at(t)], now_v[2, at(t)])
            slot = far_slot(place_ref, -1 - t)
            return (far_ref[0, slot] * sigma, far_ref[1, slot], far_ref[2, slot])

        outer = normal_stress(strain_parts(field(-2), field(-1), field(0), tools), far_ref[3, 0], far_ref[3, 1])
        lame, shear = lame_v[at(0)], shear_v[at(0)]
        parts = strain_parts(field(-1), field(0), field(1), tools)
        normal = normal_stress(parts, lame, shear)
        force = cross_force(parts, normal, lame, shear, tools)
        for b in range(3):
            far_next[b] = next_v[b, 0] + scale_v[0] * (force[b] - outer[b])
            far_next[3 + b] = next_v[b, 1] - scale_v[1] * normal[b]

    (far_next,) = call(
        far_first,
        [(6, *plane)],
        (now_v, lame_v, shear_v, scale_v, next_v, far_in),
        [VM] * 6,
        [VM],
    )
    far_next_in = lax.ppermute(far_next, "blk", far)

    def second(now_v, fwd_v, lame_v, shear_v, scale_v, next_v, terms_v, far_next_ref, near_next_ref,
        near_ref, far_ref, far_fwd_ref,
        final_v, total_v, slope_v, keep_ref, send_ref, normal_v,
    ):
        place_ref = where()
        sigma = sign(place_ref)
        tools = difference_tools(*plane)

        def at(t):
            return layer(place_ref, t)

        def start(t):
            if t >= 0:
                return (now_v[0, at(t)] * sigma, now_v[1, at(t)], now_v[2, at(t)])
            slot = far_slot(place_ref, 0)
            return (far_ref[0, slot] * sigma, far_ref[1, slot], far_ref[2, slot])

        def field(t):
            if t < 2:
                return tuple(far_next_ref[3 * t + b] for b in range(3))
            if t <= last:
                return tuple(next_v[b, t] for b in range(3))
            base = 3 * (t - cells)
            return (-near_next_ref[base], near_next_ref[base + 1], near_next_ref[base + 2])

        def fwd(k, t):
            if t < 0:
                return (far_fwd_ref[k, 0] * sigma, far_fwd_ref[k, 1], far_fwd_ref[k, 2])
            if t <= last:
                return (fwd_v[k, 0, at(t)] * sigma, fwd_v[k, 1, at(t)], fwd_v[k, 2, at(t)])
            return (near_ref[4, k] * sigma, near_ref[5, k], near_ref[6, k])

        for t in range(1, cells + 1):
            parts = strain_parts(field(t - 1), field(t), field(t + 1), tools)
            if t <= last:
                lame, shear = lame_v[at(t)], shear_v[at(t)]
            else:
                lame, shear = near_ref[3, 0], near_ref[3, 1]
            normal = normal_stress(parts, lame, shear)
            for b in range(3):
                normal_v[b, t] = normal[b]
            if t <= last:
                force = cross_force(parts, normal, lame, shear, tools)
                for b in range(3):
                    final_v[b, t] = force[b]
                if t in middle:
                    other = strain_parts(fwd(1, t - 1), fwd(1, t), fwd(1, t + 1), tools)
                    pair = term_pair(parts, other, lame, shear)
                    for k in range(2):
                        total_v[k, t] = terms_v[k, t] + pair[k]
        for t in range(cells):
            for b in range(3):
                force = normal_v[b, t + 1]
                if t > 0:
                    force = force + final_v[b, t]
                if t > 1:
                    force = force - normal_v[b, t - 1]
                old = now_v[b, at(t)]
                if b == 0:
                    old = old * sigma
                final_v[b, t] = 2.0 * field(t)[b] - old + scale_v[t] * force
        split(place_ref, total_v, middle, keep_ref, send_ref)
        parts = strain_parts(start(-1), start(0), start(1), tools)
        other = strain_parts(fwd(0, -1), fwd(0, 0), fwd(0, 1), tools)
        lame, shear = lame_v[at(0)], shear_v[at(0)]
        pair = term_pair(parts, other, lame, shear)
        empty = jnp.zeros(plane, jnp.float32)
        parts = strain_parts((empty, empty, empty), field(0), field(1), tools)
        other = strain_parts(fwd(1, -1), fwd(1, 0), fwd(1, 1), tools)
        rest = term_pair(parts, other, lame, shear)
        for k in range(2):
            total_v[k, 0] = pair[k] + rest[k]
        slope_v[0] = shear * ((0.5 * time_step) * other[0] - (time_step / 6.0) * other[6])
        slope_v[1] = (0.25 * time_step) * shear * other[3]
        slope_v[2] = (0.25 * time_step) * shear * other[4]
        slope_v[3] = (0.25 * time_step) * (lame + (2.0 / 3.0) * shear) * other[6]

    final_v, total_v, slope_v, keep_mid, send_mid = call(
        second,
        [now.shape, (2, cells, *plane), (4, *plane),
         (2, len(middle), band, lanes), (events - 1, 2, len(middle), band, lanes)],
        (now_v, fwd_v, lame_v, shear_v, scale_v, next_v, terms_v, far_next, near_next_in,
         near_in, far_in, far_fwd_in),
        [VM] * 12,
        [VM] * 5,
        [pltpu.VMEM((3, cells + 1, *plane), jnp.float32)],
    )
    shared_mid = [lax.ppermute(send_mid[i], "event", others[i]) for i in range(events - 1)]

    def far_terms(total_ref, slope_ref, far_next_in_ref, keep_ref, send_ref, total_v):
        place_ref = where()
        outer = (-far_next_in_ref[0], far_next_in_ref[1], far_next_in_ref[2])
        shear_part = total_ref[0, 0]
        for b in range(3):
            shear_part = shear_part + slope_ref[b] * outer[b]
        total_v[0, 0] = shear_part
        total_v[1, 0] = total_ref[1, 0] + slope_ref[3] * outer[0]
        split(place_ref, total_v, [0], keep_ref, send_ref)

    far_keep, far_send = call(
        far_terms,
        [(2, 1, band, lanes), (events - 1, 2, 1, band, lanes)],
        (total_v, slope_v, far_next_in),
        [VM] * 3,
        [VM] * 2,
        [pltpu.VMEM((2, 1, *plane), jnp.float32)],
    )
    far_shared = [lax.ppermute(far_send[i], "event", others[i]) for i in range(events - 1)]

    def far_second(lame_v, shear_v, scale_v, final_v, far_next_ref, next_v, far_ref, far_next_in_ref, out_ref
    ):
        place_ref = where()
        sigma = sign(place_ref)
        tools = difference_tools(*plane)

        def at(t):
            return layer(place_ref, t)

        def field(t):
            if t < 0:
                base = 3 * (-1 - t)
                return (-far_next_in_ref[base], far_next_in_ref[base + 1], far_next_in_ref[base + 2])
            return tuple(far_next_ref[3 * t + b] for b in range(3))

        outer = normal_stress(strain_parts(field(-2), field(-1), field(0), tools), far_ref[3, 0], far_ref[3, 1])
        lame, shear = lame_v[at(0)], shear_v[at(0)]
        parts = strain_parts(field(-1), field(0), field(1), tools)
        normal = normal_stress(parts, lame, shear)
        force = cross_force(parts, normal, lame, shear, tools)
        for t in range(cells):
            for b in range(3):
                value = final_v[b, t]
                if t == 0:
                    value = value + scale_v[0] * (force[b] - outer[b])
                if t == 1:
                    value = value - scale_v[1] * normal[b]
                if b == 0:
                    value = value * sigma
                out_ref[b, at(t)] = value

    (result,) = call(
        far_second,
        [now.shape],
        (lame_v, shear_v, scale_v, final_v, far_next, next_v, far_in, far_next_in),
        [VM] * 8,
        [None],
    )

    def finish(*rest):
        place_ref = where()
        width = events
        outs = rest[3 * width :]
        for group, layers in enumerate((early, middle, [0])):
            parts = rest[group * width : (group + 1) * width]
            for k in range(2):
                for i, t in enumerate(layers):
                    value = parts[0][k, i]
                    for part in parts[1:]:
                        value = value + part[k, i]
                    outs[k][layer(place_ref, t)] = value

    band_shear, band_bulk = call(
        finish,
        [(cells, band, lanes)] * 2,
        (keep, *shared, keep_mid, *shared_mid, far_keep, *far_shared),
        [VM] * (3 * events),
        [None] * 2,
    )
    return (result[None], band_shear, band_bulk)


def solution(mesh):
    in_specs = (
        P("event", None, "blk", None, None),
        P("event", None, "blk", None, None),
        P("event", None, None, "blk", None, None),
        P("blk", None, None),
        P("blk", None, None),
        P("blk", None, None),
    )
    out_specs = (
        P("event", None, "blk", None, None),
        P("blk", "event", None),
        P("blk", "event", None),
    )
    return jax.shard_map(local, mesh=mesh, in_specs=in_specs, out_specs=out_specs, check_vma=False)
```

```python
import jax
import jax.numpy as jnp
from jax import lax
from jax.experimental import pallas as pl
from jax.experimental.pallas import tpu as pltpu
from jax.sharding import PartitionSpec as P

time_step = 0.3
step_squared = time_step * time_step


def difference_tools(rows, lanes):
    row = lax.broadcasted_iota(jnp.int32, (rows, lanes), 0)
    lane = lax.broadcasted_iota(jnp.int32, (rows, lanes), 1)

    def along_rows(values):
        upper = jnp.where(row == rows - 1, 0.0, pltpu.roll(values, rows - 1, 0))
        lower = jnp.where(row == 0, 0.0, pltpu.roll(values, 1, 0))
        return upper - lower

    def along_lanes(values):
        upper = jnp.where(lane == lanes - 1, 0.0, pltpu.roll(values, lanes - 1, 1))
        lower = jnp.where(lane == 0, 0.0, pltpu.roll(values, 1, 1))
        return upper - lower

    key = lax.broadcasted_iota(jnp.int32, (3 * lanes, lanes), 0) % lanes
    out = lax.broadcasted_iota(jnp.int32, (3 * lanes, lanes), 1)
    weights = ((key == out + 1).astype(jnp.float32) - (key == out - 1).astype(jnp.float32)).astype(jnp.bfloat16)

    def along_lanes_three(fields):
        values = jnp.concatenate(fields, axis=0)
        high = values.astype(jnp.bfloat16)
        rest = values - high.astype(jnp.float32)
        middle = rest.astype(jnp.bfloat16)
        low = (rest - middle.astype(jnp.float32)).astype(jnp.bfloat16)
        parts = jnp.concatenate([high, middle, low], axis=1)
        result = jnp.dot(parts, weights, preferred_element_type=jnp.float32)
        return [result[rows * b : rows * (b + 1)] for b in range(len(fields))]

    return along_rows, along_lanes, along_lanes_three


def strain_parts(before, middle, after, tools):
    along_rows, along_lanes, along_lanes_three = tools
    first = after[0] - before[0]
    second = along_rows(middle[1])
    third = along_lanes(middle[2])
    pair_12 = (after[1] - before[1]) + along_rows(middle[0])
    pair_13 = (after[2] - before[2]) + along_lanes(middle[0])
    pair_23 = along_rows(middle[2]) + along_lanes(middle[1])
    return (first, second, third, pair_12, pair_13, pair_23, first + second + third)


def normal_stress(parts, lame, shear):
    return (2.0 * shear * parts[0] + lame * parts[6], shear * parts[3], shear * parts[4])


def cross_force(parts, normal, lame, shear, tools):
    along_rows, along_lanes, along_lanes_three = tools
    pressure = lame * parts[6]
    twice = 2.0 * shear
    s_22 = twice * parts[1] + pressure
    s_33 = twice * parts[2] + pressure
    s_23 = shear * parts[5]
    third_of = along_lanes_three((normal[2], s_23, s_33))
    return (
        along_rows(normal[1]) + third_of[0],
        along_rows(s_22) + third_of[1],
        along_rows(s_23) + third_of[2],
    )


def term_pair(parts, other, lame, shear):
    straight = parts[0] * other[0] + parts[1] * other[1] + parts[2] * other[2]
    mixed = parts[3] * other[3] + parts[4] * other[4] + parts[5] * other[5]
    traces = parts[6] * other[6]
    shear_term = shear * (
        (-0.5 * time_step) * straight - (0.25 * time_step) * mixed + (time_step / 6.0) * traces
    )
    bulk_term = (-0.25 * time_step) * (lame + (2.0 / 3.0) * shear) * traces
    return shear_term, bulk_term


costs = {'pack': 1000000, 'inner_first': 100000000, 'near_first': 100000000, 'far_first': 10000000000, 'middle_terms': 1000000000, 'edge_terms': 10000000, 'second': 1000000000, 'far_terms': 10000000, 'store_second': 10000000, 'finish': 100000000}


def call(kernel, outs, args, in_spaces, out_spaces, scratch=(), vmem=40 << 20, aliases=None):
    shapes = [
        pltpu.VMEM(shape, jnp.float32) if space is pltpu.VMEM else jax.ShapeDtypeStruct(shape, jnp.float32)
        for shape, space in zip(outs, out_spaces)
    ]
    out_spaces = [space or pltpu.VMEM for space in out_spaces]
    return pl.pallas_call(
        kernel,
        out_shape=shapes,
        in_specs=[pl.BlockSpec(memory_space=space) for space in in_spaces],
        out_specs=[pl.BlockSpec(memory_space=space) for space in out_spaces],
        scratch_shapes=list(scratch),
        name=kernel.__name__,
        input_output_aliases=aliases or {},
        compiler_params=pltpu.CompilerParams(vmem_limit_bytes=vmem),
        cost_estimate=pl.CostEstimate(
            flops=costs.get(kernel.__name__, 1), bytes_accessed=costs.get(kernel.__name__, 1), transcendentals=0
        ),
    )(*args)


def local(adjoint_now, adjoint_prev, forward_field, density, lame_first, shear_modulus):
    slabs = lax.axis_size("blk")
    events = lax.axis_size("event")
    cells, rows, lanes = density.shape
    steps = forward_field.shape[1]
    last = cells - 1
    band = rows // events
    plane = (rows, lanes)
    VM, SM, ANY = pltpu.VMEM, pltpu.SMEM, pl.ANY

    near = [(i, i + 1 - 2 * (i % 2)) for i in range(slabs)]
    far = [(i, (i - 1 + 2 * (i % 2)) % slabs) for i in range(slabs)]
    others = [
        [(i, (i + shift) % events) for i in range(events)] for shift in range(1, events)
    ]

    in_hbm = [
        pltpu.with_memory_space_constraint(x, pltpu.HBM)
        for x in (adjoint_now[0], adjoint_prev[0], forward_field[0], density, lame_first, shear_modulus)
    ]
    now_hbm, prev, forward_hbm, density, lame_hbm, shear_hbm = in_hbm
    now, forward = adjoint_now[0], forward_field[0]

    def where():
        return lax.rem(lax.axis_index("blk"), 2), lax.axis_index("event")

    def layer(place_ref, t):
        return t + place_ref[0] * (last - 2 * t)

    def far_slot(place_ref, n):
        return (1 - n) + place_ref[0] * (2 * n - 1)

    def near_slot(place_ref, n):
        return n + place_ref[0] * (1 - 2 * n)

    def sign(place_ref):
        return (1 - 2 * place_ref[0]).astype(jnp.float32)

    def pack(now_ref, forward_ref, lame_ref, shear_ref, near_ref, far_ref, sem):
        place_ref = where()
        odd = place_ref[0]
        faces = ((far_ref, layer(place_ref, 0), odd * (cells - 2)), (near_ref, layer(place_ref, last), (1 - odd) * (cells - 2)))
        copies = []
        for out, at, low in faces:
            copies.append((now_ref.at[:, pl.ds(low, 2)], out.at[pl.ds(0, 3)]))
            copies.append((lame_ref.at[at], out.at[3, 0]))
            copies.append((shear_ref.at[at], out.at[3, 1]))
        for k in range(steps):
            copies.append((forward_ref.at[k, :, layer(place_ref, last)], near_ref.at[pl.ds(4, 3), k]))
        started = [pltpu.make_async_copy(src, dst, sem.at[i]) for i, (src, dst) in enumerate(copies)]
        for copy in started:
            copy.start()
        for copy in started:
            copy.wait()

    near_out, far_out = call(
        pack,
        [(7, 2, *plane), (4, 2, *plane)],
        (now_hbm, forward_hbm, lame_hbm, shear_hbm),
        [ANY, ANY, ANY, ANY],
        [VM, VM],
        [pltpu.SemaphoreType.DMA((6 + steps,))],
    )
    near_in = lax.ppermute(near_out, "blk", near)
    far_in = lax.ppermute(far_out, "blk", far)

    def split(place_ref, terms_ref, layers, keep_ref, send_ref):
        own = place_ref[1]
        for shift in range(events):
            target = lax.rem(own + shift, events) if shift else own
            start = pl.multiple_of(target * band, 8)
            out = send_ref.at[shift - 1] if shift else keep_ref
            for k in range(2):
                for i, t in enumerate(layers):
                    out[k, i] = terms_ref[k, t, pl.ds(start, band)]

    def inner_first(now_v, prev_ref, fwd_v, dens_ref, lame_v, shear_v,
        scale_v, next_v, terms_v, far_fwd_ref,
        prev_v, dens_v, normal_v, sem,
    ):
        place_ref = where()
        moves = [
            pltpu.make_async_copy(src, dst, sem.at[i])
            for i, (src, dst) in enumerate([(dens_ref, dens_v), (prev_ref, prev_v)])
        ]
        for move in moves:
            move.start()
        sigma = sign(place_ref)
        tools = difference_tools(*plane)

        def at(t):
            return layer(place_ref, t)

        def field(t):
            return (now_v[0, at(t)] * sigma, now_v[1, at(t)], now_v[2, at(t)])

        def fwd(k, t):
            return (fwd_v[k, 0, at(t)] * sigma, fwd_v[k, 1, at(t)], fwd_v[k, 2, at(t)])

        for k in range(steps):
            for b in range(3):
                far_fwd_ref[k, b] = fwd_v[k, b, at(0)]
        for t in range(1, last):
            parts = strain_parts(field(t - 1), field(t), field(t + 1), tools)
            lame, shear = lame_v[at(t)], shear_v[at(t)]
            normal = normal_stress(parts, lame, shear)
            force = cross_force(parts, normal, lame, shear, tools)
            for b in range(3):
                normal_v[b, t] = normal[b]
                next_v[b, t] = force[b]
            other = strain_parts(fwd(0, t - 1), fwd(0, t), fwd(0, t + 1), tools)
            pair = term_pair(parts, other, lame, shear)
            terms_v[0, t] = pair[0]
            terms_v[1, t] = pair[1]
        for move in moves:
            move.wait()
        for t in range(cells):
            scale_v[t] = (0.25 * step_squared) / dens_v[at(t)]
        for t in range(cells):
            for b in range(3):
                force = None
                if 0 < t < last:
                    force = next_v[b, t]
                if t < last - 1:
                    force = normal_v[b, t + 1] if force is None else force + normal_v[b, t + 1]
                if t > 1:
                    force = -normal_v[b, t - 1] if force is None else force - normal_v[b, t - 1]
                old = prev_v[b, at(t)]
                if b == 0:
                    old = old * sigma
                next_v[b, t] = 2.0 * field(t)[b] - old + scale_v[t] * force
        for t in range(3, last - 2):
            fields = [tuple(next_v[b, t + d] for b in range(3)) for d in (-1, 0, 1)]
            parts = strain_parts(*fields, tools)
            other = strain_parts(fwd(1, t - 1), fwd(1, t), fwd(1, t + 1), tools)
            pair = term_pair(parts, other, lame_v[at(t)], shear_v[at(t)])
            for k in range(2):
                terms_v[k, t] = terms_v[k, t] + pair[k]

    now_v, fwd_v, lame_v, shear_v = now, forward, lame_first, shear_modulus
    scale_v, next_v, terms_v, far_fwd_out = call(
        inner_first,
        [density.shape, now.shape, (2, last, *plane), (steps, 3, *plane)],
        (now, prev, forward, density, lame_first, shear_modulus),
        [VM, ANY, VM, ANY, VM, VM],
        [VM] * 4,
        [pltpu.VMEM(now.shape, jnp.float32), pltpu.VMEM(density.shape, jnp.float32),
         pltpu.VMEM((3, last, *plane), jnp.float32), pltpu.SemaphoreType.DMA((2,))],
    )

    far_fwd_in = lax.ppermute(far_fwd_out, "blk", far)

    early = list(range(3, last))
    middle = [1, 2, last]

    def near_first(now_v, fwd_v, lame_v, shear_v, scale_v, next_v, terms_v, near_ref,
        near_next, near_terms, keep_ref, send_ref,
        total_v,
    ):
        place_ref = where()
        sigma = sign(place_ref)
        tools = difference_tools(*plane)

        def at(t):
            return layer(place_ref, t)

        def field(t):
            if t <= last:
                return (now_v[0, at(t)] * sigma, now_v[1, at(t)], now_v[2, at(t)])
            slot = near_slot(place_ref, t - cells)
            return (near_ref[0, slot] * sigma, near_ref[1, slot], near_ref[2, slot])

        def fwd(k, t):
            if t <= last:
                return (fwd_v[k, 0, at(t)] * sigma, fwd_v[k, 1, at(t)], fwd_v[k, 2, at(t)])
            return (near_ref[4, k] * sigma, near_ref[5, k], near_ref[6, k])

        def new(t):
            if t < last - 1:
                return tuple(next_v[b, t] for b in range(3))
            return tuple(near_next[3 * (last - t) + b] for b in range(3))

        outer = normal_stress(
            strain_parts(field(last), field(cells), field(cells + 1), tools), near_ref[3, 0], near_ref[3, 1]
        )
        lame, shear = lame_v[at(last)], shear_v[at(last)]
        parts = strain_parts(field(last - 1), field(last), field(cells), tools)
        normal = normal_stress(parts, lame, shear)
        force = cross_force(parts, normal, lame, shear, tools)
        for b in range(3):
            near_next[b] = next_v[b, last] + scale_v[last] * (force[b] + outer[b])
            near_next[3 + b] = next_v[b, last - 1] + scale_v[last - 1] * normal[b]
        other = strain_parts(fwd(0, last - 1), fwd(0, last), fwd(0, cells), tools)
        pair = term_pair(parts, other, lame, shear)
        for k in range(2):
            near_terms[k] = pair[k]
            for t in range(3, last - 2):
                total_v[k, t] = terms_v[k, t]
        for t in range(last - 2, last):
            parts = strain_parts(new(t - 1), new(t), new(t + 1), tools)
            other = strain_parts(fwd(1, t - 1), fwd(1, t), fwd(1, t + 1), tools)
            pair = term_pair(parts, other, lame_v[at(t)], shear_v[at(t)])
            for k in range(2):
                total_v[k, t] = terms_v[k, t] + pair[k]
        split(place_ref, total_v, early, keep_ref, send_ref)

    near_next, near_terms, keep, send = call(
        near_first,
        [(6, *plane), (2, *plane), (2, len(early), band, lanes), (events - 1, 2, len(early), band, lanes)],
        (now_v, fwd_v, lame_v, shear_v, scale_v, next_v, terms_v, near_in),
        [VM] * 8,
        [VM] * 4,
        [pltpu.VMEM((2, cells, *plane), jnp.float32)],
    )
    near_next_in = lax.ppermute(near_next, "blk", near)
    shared = [lax.ppermute(send[i], "event", others[i]) for i in range(events - 1)]

    def far_first(now_v, lame_v, shear_v, scale_v, next_v, far_ref, after_ref, far_next, far_after):
        place_ref = where()
        sigma = sign(place_ref)
        tools = difference_tools(*plane)

        def at(t):
            return layer(place_ref, t)

        def field(t):
            if t >= 0:
                return (now_v[0, at(t)] * sigma, now_v[1, at(t)], now_v[2, at(t)])
            slot = far_slot(place_ref, -1 - t)
            return (far_ref[0, slot] * sigma, far_ref[1, slot], far_ref[2, slot])

        outer = normal_stress(strain_parts(field(-2), field(-1), field(0), tools), far_ref[3, 0], far_ref[3, 1])
        lame, shear = lame_v[at(0)], shear_v[at(0)]
        parts = strain_parts(field(-1), field(0), field(1), tools)
        normal = normal_stress(parts, lame, shear)
        force = cross_force(parts, normal, lame, shear, tools)
        for b in range(3):
            far_next[b] = next_v[b, 0] + scale_v[0] * (force[b] - outer[b])
            far_after[b] = next_v[b, 1] - scale_v[1] * normal[b]

    far_next, far_after = call(
        far_first,
        [(3, *plane), (3, *plane)],
        (now_v, lame_v, shear_v, scale_v, next_v, far_in, near_next),
        [VM] * 7,
        [VM] * 2,
    )
    far_next_in = lax.ppermute(far_next, "blk", far)
    far_after_in = lax.ppermute(far_after, "blk", far)

    def middle_terms(fwd_v, lame_v, shear_v, next_v, near_next_v, terms_v, near_terms, far_next_ref, far_after_ref, near_next_ref, near_ref,
        keep_ref, send_ref, total_v,
    ):
        place_ref = where()
        sigma = sign(place_ref)
        tools = difference_tools(*plane)

        def at(t):
            return layer(place_ref, t)

        def field(t):
            if t < 2:
                return tuple((far_after_ref if t else far_next_ref)[b] for b in range(3))
            if t < last - 1:
                return tuple(next_v[b, t] for b in range(3))
            if t <= last:
                return tuple(near_next_v[3 * (last - t) + b] for b in range(3))
            base = 3 * (t - cells)
            return (-near_next_ref[base], near_next_ref[base + 1], near_next_ref[base + 2])

        def fwd(k, t):
            if t <= last:
                return (fwd_v[k, 0, at(t)] * sigma, fwd_v[k, 1, at(t)], fwd_v[k, 2, at(t)])
            return (near_ref[4, k] * sigma, near_ref[5, k], near_ref[6, k])

        for t in middle:
            parts = strain_parts(field(t - 1), field(t), field(t + 1), tools)
            other = strain_parts(fwd(1, t - 1), fwd(1, t), fwd(1, t + 1), tools)
            pair = term_pair(parts, other, lame_v[at(t)], shear_v[at(t)])
            for k in range(2):
                total_v[k, t] = (near_terms[k] if t == last else terms_v[k, t]) + pair[k]
        split(place_ref, total_v, middle, keep_ref, send_ref)

    keep_mid, send_mid = call(
        middle_terms,
        [(2, len(middle), band, lanes), (events - 1, 2, len(middle), band, lanes)],
        (fwd_v, lame_v, shear_v, next_v, near_next, terms_v, near_terms, far_next, far_after, near_next_in, near_in),
        [VM] * 11,
        [VM] * 2,
        [pltpu.VMEM((2, cells, *plane), jnp.float32)],
    )
    shared_mid = [lax.ppermute(send_mid[i], "event", others[i]) for i in range(events - 1)]

    def edge_terms(now_v, fwd_v, lame_v, shear_v, far_next_ref, far_after_ref, far_ref, far_fwd_ref, after_ref,
        total_v, slope_v,
    ):
        place_ref = where()
        sigma = sign(place_ref)
        tools = difference_tools(*plane)

        def at(t):
            return layer(place_ref, t)

        def start(t):
            if t >= 0:
                return (now_v[0, at(t)] * sigma, now_v[1, at(t)], now_v[2, at(t)])
            slot = far_slot(place_ref, 0)
            return (far_ref[0, slot] * sigma, far_ref[1, slot], far_ref[2, slot])

        def field(t):
            return tuple((far_after_ref if t else far_next_ref)[b] for b in range(3))

        def fwd(k, t):
            if t < 0:
                return (far_fwd_ref[k, 0] * sigma, far_fwd_ref[k, 1], far_fwd_ref[k, 2])
            return (fwd_v[k, 0, at(t)] * sigma, fwd_v[k, 1, at(t)], fwd_v[k, 2, at(t)])

        parts = strain_parts(start(-1), start(0), start(1), tools)
        other = strain_parts(fwd(0, -1), fwd(0, 0), fwd(0, 1), tools)
        lame, shear = lame_v[at(0)], shear_v[at(0)]
        pair = term_pair(parts, other, lame, shear)
        empty = jnp.zeros(plane, jnp.float32)
        parts = strain_parts((empty, empty, empty), field(0), field(1), tools)
        other = strain_parts(fwd(1, -1), fwd(1, 0), fwd(1, 1), tools)
        rest = term_pair(parts, other, lame, shear)
        for k in range(2):
            total_v[k] = pair[k] + rest[k]
        slope_v[0] = shear * ((0.5 * time_step) * other[0] - (time_step / 6.0) * other[6])
        slope_v[1] = (0.25 * time_step) * shear * other[3]
        slope_v[2] = (0.25 * time_step) * shear * other[4]
        slope_v[3] = (0.25 * time_step) * (lame + (2.0 / 3.0) * shear) * other[6]

    total_v, slope_v = call(
        edge_terms,
        [(2, *plane), (4, *plane)],
        (now_v, fwd_v, lame_v, shear_v, far_next, far_after, far_in, far_fwd_in, keep_mid),
        [VM] * 9,
        [VM] * 2,
    )

    def far_terms(total_ref, slope_ref, far_next_in_ref, keep_ref, send_ref, total_v):
        place_ref = where()
        outer = (-far_next_in_ref[0], far_next_in_ref[1], far_next_in_ref[2])
        shear_part = total_ref[0]
        for b in range(3):
            shear_part = shear_part + slope_ref[b] * outer[b]
        total_v[0, 0] = shear_part
        total_v[1, 0] = total_ref[1] + slope_ref[3] * outer[0]
        split(place_ref, total_v, [0], keep_ref, send_ref)

    far_keep, far_send = call(
        far_terms,
        [(2, 1, band, lanes), (events - 1, 2, 1, band, lanes)],
        (total_v, slope_v, far_next_in),
        [VM] * 3,
        [VM] * 2,
        [pltpu.VMEM((2, 1, *plane), jnp.float32)],
    )
    far_shared = [lax.ppermute(far_send[i], "event", others[i]) for i in range(events - 1)]

    def second(now_v, lame_v, shear_v, scale_v, next_v, near_next_v, far_next_ref, far_after_ref, near_next_ref,
        near_ref, after_ref,
        final_v, face_v, normal_v, cross_v,
    ):
        place_ref = where()
        sigma = sign(place_ref)
        tools = difference_tools(*plane)

        def at(t):
            return layer(place_ref, t)

        def field(t):
            if t < 2:
                return tuple((far_after_ref if t else far_next_ref)[b] for b in range(3))
            if t < last - 1:
                return tuple(next_v[b, t] for b in range(3))
            if t <= last:
                return tuple(near_next_v[3 * (last - t) + b] for b in range(3))
            base = 3 * (t - cells)
            return (-near_next_ref[base], near_next_ref[base + 1], near_next_ref[base + 2])

        for t in range(1, cells + 1):
            parts = strain_parts(field(t - 1), field(t), field(t + 1), tools)
            if t <= last:
                lame, shear = lame_v[at(t)], shear_v[at(t)]
            else:
                lame, shear = near_ref[3, 0], near_ref[3, 1]
            normal = normal_stress(parts, lame, shear)
            for b in range(3):
                normal_v[b, t] = normal[b]
            if t <= last:
                force = cross_force(parts, normal, lame, shear, tools)
                for b in range(3):
                    cross_v[b, t] = force[b]
        for t in range(cells):
            for b in range(3):
                force = normal_v[b, t + 1]
                if t > 0:
                    force = force + cross_v[b, t]
                if t > 1:
                    force = force - normal_v[b, t - 1]
                old = now_v[b, at(t)]
                if b == 0:
                    old = old * sigma
                value = 2.0 * field(t)[b] - old + scale_v[t] * force
                if t < 2:
                    face_v[b, t] = value
                else:
                    final_v[b, at(t)] = value * sigma if b == 0 else value

    final_v, face_v = call(
        second,
        [now.shape, (3, 2, *plane)],
        (now_v, lame_v, shear_v, scale_v, next_v, near_next, far_next, far_after, near_next_in,
         near_in, far_keep),
        [VM] * 11,
        [VM] * 2,
        [pltpu.VMEM((3, cells + 1, *plane), jnp.float32), pltpu.VMEM(now.shape, jnp.float32)],
    )

    def store_second(final_v, out_ref, sem):
        place_ref = where()
        inner = pl.ds(2 - 2 * place_ref[0], cells - 2)
        copy = pltpu.make_async_copy(final_v.at[:, inner], out_ref.at[:, inner], sem)
        copy.start()
        copy.wait()

    (result,) = call(
        store_second, [now.shape], (final_v,), [VM], [ANY], [pltpu.SemaphoreType.DMA(())]
    )

    def finish(result_ref, lame_v, shear_v, scale_v, face_v, far_next_ref, far_after_ref, far_ref,
        far_next_in_ref, far_after_in_ref, *rest,
    ):
        pieces, (out_ref, *band_refs, edge_v, band_v, sem) = rest[: 3 * events], rest[3 * events :]
        place_ref = where()
        sigma = sign(place_ref)
        tools = difference_tools(*plane)

        def at(t):
            return layer(place_ref, t)

        def field(t):
            if t < 0:
                come = far_next_in_ref if t == -1 else far_after_in_ref
                return (-come[0], come[1], come[2])
            return tuple((far_after_ref if t else far_next_ref)[b] for b in range(3))

        outer = normal_stress(strain_parts(field(-2), field(-1), field(0), tools), far_ref[3, 0], far_ref[3, 1])
        lame, shear = lame_v[at(0)], shear_v[at(0)]
        parts = strain_parts(field(-1), field(0), field(1), tools)
        normal = normal_stress(parts, lame, shear)
        force = cross_force(parts, normal, lame, shear, tools)
        odd = place_ref[0]
        for b in range(3):
            first = face_v[b, 0] + scale_v[0] * (force[b] - outer[b])
            after = face_v[b, 1] - scale_v[1] * normal[b]
            edge_v[b, odd] = first * sigma if b == 0 else first
            edge_v[b, 1 - odd] = after * sigma if b == 0 else after
        copies = [pltpu.make_async_copy(edge_v, out_ref.at[:, pl.ds(odd * (cells - 2), 2)], sem.at[0])]
        copies[0].start()
        for k in range(2):
            for i, layers in enumerate((early, middle, [0])):
                own, *others_parts = pieces[i * events : (i + 1) * events]
                for j, t in enumerate(layers):
                    value = own[k, j]
                    for part in others_parts:
                        value = value + part[k, j]
                    band_v[k, at(t)] = value
            copies.append(pltpu.make_async_copy(band_v.at[k], band_refs[k], sem.at[1 + k]))
            copies[-1].start()
        for copy in copies:
            copy.wait()

    result, band_shear, band_bulk = call(
        finish,
        [now.shape, (cells, band, lanes), (cells, band, lanes)],
        (result, lame_v, shear_v, scale_v, face_v, far_next, far_after, far_in, far_next_in, far_after_in,
         keep, *shared, keep_mid, *shared_mid, far_keep, *far_shared),
        [ANY] + [VM] * (9 + 3 * events),
        [ANY] * 3,
        [pltpu.VMEM((3, 2, *plane), jnp.float32), pltpu.VMEM((2, cells, band, lanes), jnp.float32),
         pltpu.SemaphoreType.DMA((3,))],
        aliases={0: 0},
    )
    return (result[None], band_shear, band_bulk)


def solution(mesh):
    in_specs = (
        P("event", None, "blk", None, None),
        P("event", None, "blk", None, None),
        P("event", None, None, "blk", None, None),
        P("blk", None, None),
        P("blk", None, None),
        P("blk", None, None),
    )
    out_specs = (
        P("event", None, "blk", None, None),
        P("blk", "event", None),
        P("blk", "event", None),
    )
    return jax.shard_map(local, mesh=mesh, in_specs=in_specs, out_specs=out_specs, check_vma=False)
```

```python
import jax
import jax.numpy as jnp
from jax import lax
from jax.experimental import pallas as pl
from jax.experimental.pallas import tpu as pltpu
from jax.sharding import PartitionSpec as P

time_step = 0.3
step_squared = time_step * time_step


def difference_tools(rows, lanes):
    row = lax.broadcasted_iota(jnp.int32, (rows, lanes), 0)
    lane = lax.broadcasted_iota(jnp.int32, (rows, lanes), 1)

    def along_rows(values):
        upper = jnp.where(row == rows - 1, 0.0, pltpu.roll(values, rows - 1, 0))
        lower = jnp.where(row == 0, 0.0, pltpu.roll(values, 1, 0))
        return upper - lower

    def along_lanes(values):
        upper = jnp.where(lane == lanes - 1, 0.0, pltpu.roll(values, lanes - 1, 1))
        lower = jnp.where(lane == 0, 0.0, pltpu.roll(values, 1, 1))
        return upper - lower

    key = lax.broadcasted_iota(jnp.int32, (3 * lanes, lanes), 0) % lanes
    out = lax.broadcasted_iota(jnp.int32, (3 * lanes, lanes), 1)
    weights = ((key == out + 1).astype(jnp.float32) - (key == out - 1).astype(jnp.float32)).astype(jnp.bfloat16)

    def along_lanes_three(fields):
        values = jnp.concatenate(fields, axis=0)
        high = values.astype(jnp.bfloat16)
        rest = values - high.astype(jnp.float32)
        middle = rest.astype(jnp.bfloat16)
        low = (rest - middle.astype(jnp.float32)).astype(jnp.bfloat16)
        parts = jnp.concatenate([high, middle, low], axis=1)
        result = jnp.dot(parts, weights, preferred_element_type=jnp.float32)
        return [result[rows * b : rows * (b + 1)] for b in range(len(fields))]

    return along_rows, along_lanes, along_lanes_three


def strain_parts(before, middle, after, tools):
    along_rows, along_lanes, along_lanes_three = tools
    first = after[0] - before[0]
    second = along_rows(middle[1])
    third = along_lanes(middle[2])
    pair_12 = (after[1] - before[1]) + along_rows(middle[0])
    pair_13 = (after[2] - before[2]) + along_lanes(middle[0])
    pair_23 = along_rows(middle[2]) + along_lanes(middle[1])
    return (first, second, third, pair_12, pair_13, pair_23, first + second + third)


def normal_stress(parts, lame, shear):
    return (2.0 * shear * parts[0] + lame * parts[6], shear * parts[3], shear * parts[4])


def cross_force(parts, normal, lame, shear, tools):
    along_rows, along_lanes, along_lanes_three = tools
    pressure = lame * parts[6]
    twice = 2.0 * shear
    s_22 = twice * parts[1] + pressure
    s_33 = twice * parts[2] + pressure
    s_23 = shear * parts[5]
    third_of = along_lanes_three((normal[2], s_23, s_33))
    return (
        along_rows(normal[1]) + third_of[0],
        along_rows(s_22) + third_of[1],
        along_rows(s_23) + third_of[2],
    )


def term_pair(parts, other, lame, shear):
    straight = parts[0] * other[0] + parts[1] * other[1] + parts[2] * other[2]
    mixed = parts[3] * other[3] + parts[4] * other[4] + parts[5] * other[5]
    traces = parts[6] * other[6]
    shear_term = shear * (
        (-0.5 * time_step) * straight - (0.25 * time_step) * mixed + (time_step / 6.0) * traces
    )
    bulk_term = (-0.25 * time_step) * (lame + (2.0 / 3.0) * shear) * traces
    return shear_term, bulk_term


costs = {'pack': 1000000000, 'inner_first': 1000000000, 'near_first': 1000000, 'far_first': 10000000000, 'middle_terms': 10000000, 'edge_terms': 10000000, 'second': 100000000, 'far_terms': 10000000000, 'store_second': 100000000, 'far_second': 10000000000, 'finish': 100000}


def call(kernel, outs, args, in_spaces, out_spaces, scratch=(), vmem=40 << 20, aliases=None):
    shapes = [
        pltpu.VMEM(shape, jnp.float32) if space is pltpu.VMEM else jax.ShapeDtypeStruct(shape, jnp.float32)
        for shape, space in zip(outs, out_spaces)
    ]
    out_spaces = [space or pltpu.VMEM for space in out_spaces]
    return pl.pallas_call(
        kernel,
        out_shape=shapes,
        in_specs=[pl.BlockSpec(memory_space=space) for space in in_spaces],
        out_specs=[pl.BlockSpec(memory_space=space) for space in out_spaces],
        scratch_shapes=list(scratch),
        name=kernel.__name__,
        input_output_aliases=aliases or {},
        compiler_params=pltpu.CompilerParams(vmem_limit_bytes=vmem),
        cost_estimate=pl.CostEstimate(
            flops=costs.get(kernel.__name__, 1), bytes_accessed=costs.get(kernel.__name__, 1), transcendentals=0
        ),
    )(*args)


def local(adjoint_now, adjoint_prev, forward_field, density, lame_first, shear_modulus):
    slabs = lax.axis_size("blk")
    events = lax.axis_size("event")
    cells, rows, lanes = density.shape
    steps = forward_field.shape[1]
    last = cells - 1
    band = rows // events
    plane = (rows, lanes)
    VM, SM, ANY = pltpu.VMEM, pltpu.SMEM, pl.ANY

    near = [(i, i + 1 - 2 * (i % 2)) for i in range(slabs)]
    far = [(i, (i - 1 + 2 * (i % 2)) % slabs) for i in range(slabs)]
    others = [
        [(i, (i + shift) % events) for i in range(events)] for shift in range(1, events)
    ]

    in_hbm = [
        pltpu.with_memory_space_constraint(x, pltpu.HBM)
        for x in (adjoint_now[0], adjoint_prev[0], forward_field[0], density, lame_first, shear_modulus)
    ]
    now_hbm, prev, forward_hbm, density, lame_hbm, shear_hbm = in_hbm
    now, forward = adjoint_now[0], forward_field[0]

    def where():
        return lax.rem(lax.axis_index("blk"), 2), lax.axis_index("event")

    def layer(place_ref, t):
        return t + place_ref[0] * (last - 2 * t)

    def far_slot(place_ref, n):
        return (1 - n) + place_ref[0] * (2 * n - 1)

    def near_slot(place_ref, n):
        return n + place_ref[0] * (1 - 2 * n)

    def sign(place_ref):
        return (1 - 2 * place_ref[0]).astype(jnp.float32)

    def pack(now_ref, forward_ref, lame_ref, shear_ref, near_ref, near_model_ref, near_fwd_ref, far_ref, sem):
        place_ref = where()
        odd = place_ref[0]
        at, low = layer(place_ref, 0), odd * (cells - 2)
        copies = [
            (now_ref.at[:, pl.ds(low, 2)], far_ref.at[pl.ds(0, 3)]),
            (lame_ref.at[at], far_ref.at[3, 0]),
            (shear_ref.at[at], far_ref.at[3, 1]),
        ]
        at, low = layer(place_ref, last), (1 - odd) * (cells - 2)
        copies.append((now_ref.at[:, pl.ds(low, 2)], near_ref))
        copies.append((lame_ref.at[at], near_model_ref.at[0]))
        copies.append((shear_ref.at[at], near_model_ref.at[1]))
        copies.append((forward_ref.at[:, :, layer(place_ref, last)], near_fwd_ref))
        started = [pltpu.make_async_copy(src, dst, sem.at[i]) for i, (src, dst) in enumerate(copies)]
        for copy in started:
            copy.start()
        for copy in started:
            copy.wait()

    near_out, near_model_out, near_fwd_out, far_out = call(
        pack,
        [(3, 2, *plane), (2, *plane), (steps, 3, *plane), (4, 2, *plane)],
        (now_hbm, forward_hbm, lame_hbm, shear_hbm),
        [ANY, ANY, ANY, ANY],
        [VM] * 4,
        [pltpu.SemaphoreType.DMA((7,))],
    )
    near_in = lax.ppermute(near_out, "blk", near)
    near_model_in = lax.ppermute(near_model_out, "blk", near)
    near_fwd_in = lax.ppermute(near_fwd_out, "blk", near)
    far_in = lax.ppermute(far_out, "blk", far)

    def split(place_ref, terms_ref, layers, keep_ref, send_ref):
        own = place_ref[1]
        for shift in range(events):
            target = lax.rem(own + shift, events) if shift else own
            start = pl.multiple_of(target * band, 8)
            out = send_ref.at[shift - 1] if shift else keep_ref
            for k in range(2):
                for i, t in enumerate(layers):
                    out[k, i] = terms_ref[k, t, pl.ds(start, band)]

    def inner_first(now_v, prev_ref, fwd_v, dens_ref, lame_v, shear_v,
        scale_v, next_v, terms_v, far_fwd_ref,
        prev_v, dens_v, normal_v, sem,
    ):
        place_ref = where()
        moves = [
            pltpu.make_async_copy(src, dst, sem.at[i])
            for i, (src, dst) in enumerate([(dens_ref, dens_v), (prev_ref, prev_v)])
        ]
        for move in moves:
            move.start()
        sigma = sign(place_ref)
        tools = difference_tools(*plane)

        def at(t):
            return layer(place_ref, t)

        def field(t):
            return (now_v[0, at(t)] * sigma, now_v[1, at(t)], now_v[2, at(t)])

        def fwd(k, t):
            return (fwd_v[k, 0, at(t)] * sigma, fwd_v[k, 1, at(t)], fwd_v[k, 2, at(t)])

        for k in range(steps):
            for b in range(3):
                far_fwd_ref[k, b] = fwd_v[k, b, at(0)]
        for t in range(1, last):
            parts = strain_parts(field(t - 1), field(t), field(t + 1), tools)
            lame, shear = lame_v[at(t)], shear_v[at(t)]
            normal = normal_stress(parts, lame, shear)
            force = cross_force(parts, normal, lame, shear, tools)
            for b in range(3):
                normal_v[b, t] = normal[b]
                next_v[b, t] = force[b]
            other = strain_parts(fwd(0, t - 1), fwd(0, t), fwd(0, t + 1), tools)
            pair = term_pair(parts, other, lame, shear)
            terms_v[0, t] = pair[0]
            terms_v[1, t] = pair[1]
        for move in moves:
            move.wait()
        for t in range(cells):
            scale_v[t] = (0.25 * step_squared) / dens_v[at(t)]
        for t in range(cells):
            for b in range(3):
                force = None
                if 0 < t < last:
                    force = next_v[b, t]
                if t < last - 1:
                    force = normal_v[b, t + 1] if force is None else force + normal_v[b, t + 1]
                if t > 1:
                    force = -normal_v[b, t - 1] if force is None else force - normal_v[b, t - 1]
                old = prev_v[b, at(t)]
                if b == 0:
                    old = old * sigma
                next_v[b, t] = 2.0 * field(t)[b] - old + scale_v[t] * force

    now_v, fwd_v, lame_v, shear_v = now, forward, lame_first, shear_modulus
    scale_v, next_v, terms_v, far_fwd_out = call(
        inner_first,
        [density.shape, now.shape, (2, last, *plane), (steps, 3, *plane)],
        (now, prev, forward, density, lame_first, shear_modulus),
        [VM, ANY, VM, ANY, VM, VM],
        [VM] * 4,
        [pltpu.VMEM(now.shape, jnp.float32), pltpu.VMEM(density.shape, jnp.float32),
         pltpu.VMEM((3, last, *plane), jnp.float32), pltpu.SemaphoreType.DMA((2,))],
    )

    far_fwd_in = lax.ppermute(far_fwd_out, "blk", far)

    middle = list(range(1, cells))

    def near_first(now_v, lame_v, shear_v, scale_v, next_v, near_ref, near_model_ref, near_next):
        place_ref = where()
        sigma = sign(place_ref)
        tools = difference_tools(*plane)

        def at(t):
            return layer(place_ref, t)

        def field(t):
            if t <= last:
                return (now_v[0, at(t)] * sigma, now_v[1, at(t)], now_v[2, at(t)])
            slot = near_slot(place_ref, t - cells)
            return (near_ref[0, slot] * sigma, near_ref[1, slot], near_ref[2, slot])

        outer = normal_stress(
            strain_parts(field(last), field(cells), field(cells + 1), tools), near_model_ref[0], near_model_ref[1]
        )
        lame, shear = lame_v[at(last)], shear_v[at(last)]
        parts = strain_parts(field(last - 1), field(last), field(cells), tools)
        normal = normal_stress(parts, lame, shear)
        force = cross_force(parts, normal, lame, shear, tools)
        for b in range(3):
            near_next[b] = next_v[b, last] + scale_v[last] * (force[b] + outer[b])
            near_next[3 + b] = next_v[b, last - 1] + scale_v[last - 1] * normal[b]

    (near_next,) = call(
        near_first,
        [(6, *plane)],
        (now_v, lame_v, shear_v, scale_v, next_v, near_in, near_model_in),
        [VM] * 7,
        [VM],
    )
    near_next_in = lax.ppermute(near_next, "blk", near)

    def far_first(now_v, lame_v, shear_v, scale_v, next_v, far_ref, after_ref, far_next, far_after):
        place_ref = where()
        sigma = sign(place_ref)
        tools = difference_tools(*plane)

        def at(t):
            return layer(place_ref, t)

        def field(t):
            if t >= 0:
                return (now_v[0, at(t)] * sigma, now_v[1, at(t)], now_v[2, at(t)])
            slot = far_slot(place_ref, -1 - t)
            return (far_ref[0, slot] * sigma, far_ref[1, slot], far_ref[2, slot])

        outer = normal_stress(strain_parts(field(-2), field(-1), field(0), tools), far_ref[3, 0], far_ref[3, 1])
        lame, shear = lame_v[at(0)], shear_v[at(0)]
        parts = strain_parts(field(-1), field(0), field(1), tools)
        normal = normal_stress(parts, lame, shear)
        force = cross_force(parts, normal, lame, shear, tools)
        for b in range(3):
            far_next[b] = next_v[b, 0] + scale_v[0] * (force[b] - outer[b])
            far_after[b] = next_v[b, 1] - scale_v[1] * normal[b]

    far_next, far_after = call(
        far_first,
        [(3, *plane), (3, *plane)],
        (now_v, lame_v, shear_v, scale_v, next_v, far_in, near_next),
        [VM] * 7,
        [VM] * 2,
    )
    far_next_in = lax.ppermute(far_next, "blk", far)
    far_after_in = lax.ppermute(far_after, "blk", far)

    def middle_terms(now_v, fwd_v, lame_v, shear_v, next_v, near_next_v, terms_v, far_next_ref, far_after_ref, near_next_ref,
        near_ref, near_fwd_ref,
        keep_ref, send_ref, total_v,
    ):
        place_ref = where()
        sigma = sign(place_ref)
        tools = difference_tools(*plane)

        def at(t):
            return layer(place_ref, t)

        def field(t):
            if t < 2:
                return tuple((far_after_ref if t else far_next_ref)[b] for b in range(3))
            if t < last - 1:
                return tuple(next_v[b, t] for b in range(3))
            if t <= last:
                return tuple(near_next_v[3 * (last - t) + b] for b in range(3))
            base = 3 * (t - cells)
            return (-near_next_ref[base], near_next_ref[base + 1], near_next_ref[base + 2])

        def fwd(k, t):
            if t <= last:
                return (fwd_v[k, 0, at(t)] * sigma, fwd_v[k, 1, at(t)], fwd_v[k, 2, at(t)])
            return (near_fwd_ref[k, 0] * sigma, near_fwd_ref[k, 1], near_fwd_ref[k, 2])

        def start(t):
            if t <= last:
                return (now_v[0, at(t)] * sigma, now_v[1, at(t)], now_v[2, at(t)])
            slot = near_slot(place_ref, t - cells)
            return (near_ref[0, slot] * sigma, near_ref[1, slot], near_ref[2, slot])

        for t in middle:
            lame, shear = lame_v[at(t)], shear_v[at(t)]
            if t < last:
                total = (terms_v[0, t], terms_v[1, t])
            else:
                parts = strain_parts(start(t - 1), start(t), start(t + 1), tools)
                other = strain_parts(fwd(0, t - 1), fwd(0, t), fwd(0, t + 1), tools)
                total = term_pair(parts, other, lame, shear)
            parts = strain_parts(field(t - 1), field(t), field(t + 1), tools)
            other = strain_parts(fwd(1, t - 1), fwd(1, t), fwd(1, t + 1), tools)
            pair = term_pair(parts, other, lame, shear)
            for k in range(2):
                total_v[k, t] = total[k] + pair[k]
        split(place_ref, total_v, middle, keep_ref, send_ref)

    keep_mid, send_mid = call(
        middle_terms,
        [(2, len(middle), band, lanes), (events - 1, 2, len(middle), band, lanes)],
        (now_v, fwd_v, lame_v, shear_v, next_v, near_next, terms_v, far_next, far_after, near_next_in, near_in, near_fwd_in),
        [VM] * 12,
        [VM] * 2,
        [pltpu.VMEM((2, cells, *plane), jnp.float32)],
    )
    shared_mid = [lax.ppermute(send_mid[i], "event", others[i]) for i in range(events - 1)]

    def edge_terms(now_v, fwd_v, lame_v, shear_v, far_next_ref, far_after_ref, far_ref, far_fwd_ref, after_ref,
        total_v, slope_v,
    ):
        place_ref = where()
        sigma = sign(place_ref)
        tools = difference_tools(*plane)

        def at(t):
            return layer(place_ref, t)

        def start(t):
            if t >= 0:
                return (now_v[0, at(t)] * sigma, now_v[1, at(t)], now_v[2, at(t)])
            slot = far_slot(place_ref, 0)
            return (far_ref[0, slot] * sigma, far_ref[1, slot], far_ref[2, slot])

        def field(t):
            return tuple((far_after_ref if t else far_next_ref)[b] for b in range(3))

        def fwd(k, t):
            if t < 0:
                return (far_fwd_ref[k, 0] * sigma, far_fwd_ref[k, 1], far_fwd_ref[k, 2])
            return (fwd_v[k, 0, at(t)] * sigma, fwd_v[k, 1, at(t)], fwd_v[k, 2, at(t)])

        parts = strain_parts(start(-1), start(0), start(1), tools)
        other = strain_parts(fwd(0, -1), fwd(0, 0), fwd(0, 1), tools)
        lame, shear = lame_v[at(0)], shear_v[at(0)]
        pair = term_pair(parts, other, lame, shear)
        empty = jnp.zeros(plane, jnp.float32)
        parts = strain_parts((empty, empty, empty), field(0), field(1), tools)
        other = strain_parts(fwd(1, -1), fwd(1, 0), fwd(1, 1), tools)
        rest = term_pair(parts, other, lame, shear)
        for k in range(2):
            total_v[k] = pair[k] + rest[k]
        slope_v[0] = shear * ((0.5 * time_step) * other[0] - (time_step / 6.0) * other[6])
        slope_v[1] = (0.25 * time_step) * shear * other[3]
        slope_v[2] = (0.25 * time_step) * shear * other[4]
        slope_v[3] = (0.25 * time_step) * (lame + (2.0 / 3.0) * shear) * other[6]

    total_v, slope_v = call(
        edge_terms,
        [(2, *plane), (4, *plane)],
        (now_v, fwd_v, lame_v, shear_v, far_next, far_after, far_in, far_fwd_in, keep_mid),
        [VM] * 9,
        [VM] * 2,
    )

    def far_terms(total_ref, slope_ref, far_next_in_ref, keep_ref, send_ref, total_v):
        place_ref = where()
        outer = (-far_next_in_ref[0], far_next_in_ref[1], far_next_in_ref[2])
        shear_part = total_ref[0]
        for b in range(3):
            shear_part = shear_part + slope_ref[b] * outer[b]
        total_v[0, 0] = shear_part
        total_v[1, 0] = total_ref[1] + slope_ref[3] * outer[0]
        split(place_ref, total_v, [0], keep_ref, send_ref)

    far_keep, far_send = call(
        far_terms,
        [(2, 1, band, lanes), (events - 1, 2, 1, band, lanes)],
        (total_v, slope_v, far_next_in),
        [VM] * 3,
        [VM] * 2,
        [pltpu.VMEM((2, 1, *plane), jnp.float32)],
    )
    far_shared = [lax.ppermute(far_send[i], "event", others[i]) for i in range(events - 1)]

    def second(now_v, lame_v, shear_v, scale_v, next_v, near_next_v, far_next_ref, far_after_ref, near_next_ref,
        near_model_ref, after_ref,
        final_v, face_v, normal_v, cross_v,
    ):
        place_ref = where()
        sigma = sign(place_ref)
        tools = difference_tools(*plane)

        def at(t):
            return layer(place_ref, t)

        def field(t):
            if t < 2:
                return tuple((far_after_ref if t else far_next_ref)[b] for b in range(3))
            if t < last - 1:
                return tuple(next_v[b, t] for b in range(3))
            if t <= last:
                return tuple(near_next_v[3 * (last - t) + b] for b in range(3))
            base = 3 * (t - cells)
            return (-near_next_ref[base], near_next_ref[base + 1], near_next_ref[base + 2])

        for t in range(1, cells + 1):
            parts = strain_parts(field(t - 1), field(t), field(t + 1), tools)
            if t <= last:
                lame, shear = lame_v[at(t)], shear_v[at(t)]
            else:
                lame, shear = near_model_ref[0], near_model_ref[1]
            normal = normal_stress(parts, lame, shear)
            for b in range(3):
                normal_v[b, t] = normal[b]
            if t <= last:
                force = cross_force(parts, normal, lame, shear, tools)
                for b in range(3):
                    cross_v[b, t] = force[b]
        for t in range(cells):
            for b in range(3):
                force = normal_v[b, t + 1]
                if t > 0:
                    force = force + cross_v[b, t]
                if t > 1:
                    force = force - normal_v[b, t - 1]
                old = now_v[b, at(t)]
                if b == 0:
                    old = old * sigma
                value = 2.0 * field(t)[b] - old + scale_v[t] * force
                if t < 2:
                    face_v[b, t] = value
                else:
                    final_v[b, at(t)] = value * sigma if b == 0 else value

    final_v, face_v = call(
        second,
        [now.shape, (3, 2, *plane)],
        (now_v, lame_v, shear_v, scale_v, next_v, near_next, far_next, far_after, near_next_in,
         near_model_in, far_keep),
        [VM] * 11,
        [VM] * 2,
        [pltpu.VMEM((3, cells + 1, *plane), jnp.float32), pltpu.VMEM(now.shape, jnp.float32)],
    )

    def store_second(final_v, out_ref, sem):
        place_ref = where()
        inner = pl.ds(2 - 2 * place_ref[0], cells - 2)
        copy = pltpu.make_async_copy(final_v.at[:, inner], out_ref.at[:, inner], sem)
        copy.start()
        copy.wait()

    (result,) = call(
        store_second, [now.shape], (final_v,), [VM], [ANY], [pltpu.SemaphoreType.DMA(())]
    )

    def far_second(lame_v, shear_v, scale_v, face_v, far_next_ref, far_after_ref, far_ref,
        far_next_in_ref, far_after_in_ref, *rest,
    ):
        pieces, (edge_v, sum_ref) = rest[:events], rest[events:]
        place_ref = where()
        sigma = sign(place_ref)
        tools = difference_tools(*plane)

        def at(t):
            return layer(place_ref, t)

        def field(t):
            if t < 0:
                come = far_next_in_ref if t == -1 else far_after_in_ref
                return (-come[0], come[1], come[2])
            return tuple((far_after_ref if t else far_next_ref)[b] for b in range(3))

        outer = normal_stress(strain_parts(field(-2), field(-1), field(0), tools), far_ref[3, 0], far_ref[3, 1])
        lame, shear = lame_v[at(0)], shear_v[at(0)]
        parts = strain_parts(field(-1), field(0), field(1), tools)
        normal = normal_stress(parts, lame, shear)
        force = cross_force(parts, normal, lame, shear, tools)
        odd = place_ref[0]
        for b in range(3):
            first = face_v[b, 0] + scale_v[0] * (force[b] - outer[b])
            after = face_v[b, 1] - scale_v[1] * normal[b]
            edge_v[b, odd] = first * sigma if b == 0 else first
            edge_v[b, 1 - odd] = after * sigma if b == 0 else after
        for k in range(2):
            for j in range(len(middle)):
                value = pieces[0][k, j]
                for piece in pieces[1:]:
                    value = value + piece[k, j]
                sum_ref[k, j] = value

    edge, sum_mid = call(
        far_second,
        [(3, 2, *plane), (2, len(middle), band, lanes)],
        (lame_v, shear_v, scale_v, face_v, far_next, far_after, far_in, far_next_in, far_after_in,
         keep_mid, *shared_mid),
        [VM] * (9 + events),
        [VM] * 2,
    )

    def finish(result_ref, edge_v, *rest):
        pieces, (out_ref, *band_refs, band_v, sem) = rest[: events + 1], rest[events + 1 :]
        place_ref = where()
        copies = [
            pltpu.make_async_copy(edge_v, out_ref.at[:, pl.ds(place_ref[0] * (cells - 2), 2)], sem.at[0])
        ]
        copies[0].start()
        for k in range(2):
            groups = (([0], pieces[:events]), (middle, pieces[events:]))
            for layers, (own, *others_parts) in groups:
                for j, t in enumerate(layers):
                    value = own[k, j]
                    for part in others_parts:
                        value = value + part[k, j]
                    band_v[k, layer(place_ref, t)] = value
            copies.append(pltpu.make_async_copy(band_v.at[k], band_refs[k], sem.at[1 + k]))
            copies[-1].start()
        for copy in copies:
            copy.wait()

    result, band_shear, band_bulk = call(
        finish,
        [now.shape, (cells, band, lanes), (cells, band, lanes)],
        (result, edge, far_keep, *far_shared, sum_mid),
        [ANY] + [VM] * (2 + events),
        [ANY] * 3,
        [pltpu.VMEM((2, cells, band, lanes), jnp.float32), pltpu.SemaphoreType.DMA((3,))],
        aliases={0: 0},
    )
    return (result[None], band_shear, band_bulk)


def solution(mesh):
    in_specs = (
        P("event", None, "blk", None, None),
        P("event", None, "blk", None, None),
        P("event", None, None, "blk", None, None),
        P("blk", None, None),
        P("blk", None, None),
        P("blk", None, None),
    )
    out_specs = (
        P("event", None, "blk", None, None),
        P("blk", "event", None),
        P("blk", "event", None),
    )
    return jax.shard_map(local, mesh=mesh, in_specs=in_specs, out_specs=out_specs, check_vma=False)
```

```python
import jax
import jax.numpy as jnp
from jax import lax
from jax.experimental import pallas as pl
from jax.experimental.pallas import tpu as pltpu
from jax.sharding import PartitionSpec as P

time_step = 0.3
step_squared = time_step * time_step


def difference_tools(rows, lanes):
    row = lax.broadcasted_iota(jnp.int32, (rows, lanes), 0)
    lane = lax.broadcasted_iota(jnp.int32, (rows, lanes), 1)

    def along_rows(values):
        upper = jnp.where(row == rows - 1, 0.0, pltpu.roll(values, rows - 1, 0))
        lower = jnp.where(row == 0, 0.0, pltpu.roll(values, 1, 0))
        return upper - lower

    def along_lanes(values):
        upper = jnp.where(lane == lanes - 1, 0.0, pltpu.roll(values, lanes - 1, 1))
        lower = jnp.where(lane == 0, 0.0, pltpu.roll(values, 1, 1))
        return upper - lower

    key = lax.broadcasted_iota(jnp.int32, (3 * lanes, lanes), 0) % lanes
    out = lax.broadcasted_iota(jnp.int32, (3 * lanes, lanes), 1)
    weights = ((key == out + 1).astype(jnp.float32) - (key == out - 1).astype(jnp.float32)).astype(jnp.bfloat16)

    def along_lanes_three(fields):
        values = jnp.concatenate(fields, axis=0)
        high = values.astype(jnp.bfloat16)
        rest = values - high.astype(jnp.float32)
        middle = rest.astype(jnp.bfloat16)
        low = (rest - middle.astype(jnp.float32)).astype(jnp.bfloat16)
        parts = jnp.concatenate([high, middle, low], axis=1)
        result = jnp.dot(parts, weights, preferred_element_type=jnp.float32)
        return [result[rows * b : rows * (b + 1)] for b in range(len(fields))]

    return along_rows, along_lanes, along_lanes_three


def strain_parts(before, middle, after, tools):
    along_rows, along_lanes, along_lanes_three = tools
    first = after[0] - before[0]
    second = along_rows(middle[1])
    third = along_lanes(middle[2])
    pair_12 = (after[1] - before[1]) + along_rows(middle[0])
    pair_13 = (after[2] - before[2]) + along_lanes(middle[0])
    pair_23 = along_rows(middle[2]) + along_lanes(middle[1])
    return (first, second, third, pair_12, pair_13, pair_23, first + second + third)


def normal_stress(parts, lame, shear):
    return (2.0 * shear * parts[0] + lame * parts[6], shear * parts[3], shear * parts[4])


def cross_force(parts, normal, lame, shear, tools):
    along_rows, along_lanes, along_lanes_three = tools
    pressure = lame * parts[6]
    twice = 2.0 * shear
    s_22 = twice * parts[1] + pressure
    s_33 = twice * parts[2] + pressure
    s_23 = shear * parts[5]
    third_of = along_lanes_three((normal[2], s_23, s_33))
    return (
        along_rows(normal[1]) + third_of[0],
        along_rows(s_22) + third_of[1],
        along_rows(s_23) + third_of[2],
    )


def term_pair(parts, other, lame, shear):
    straight = parts[0] * other[0] + parts[1] * other[1] + parts[2] * other[2]
    mixed = parts[3] * other[3] + parts[4] * other[4] + parts[5] * other[5]
    traces = parts[6] * other[6]
    shear_term = shear * (
        (-0.5 * time_step) * straight - (0.25 * time_step) * mixed + (time_step / 6.0) * traces
    )
    bulk_term = (-0.25 * time_step) * (lame + (2.0 / 3.0) * shear) * traces
    return shear_term, bulk_term


costs = {'pack': 1000000000, 'inner_first': 1000000000, 'near_first': 1000000, 'far_first': 10000000000, 'middle_terms': 10000000, 'edge_terms': 10000000, 'second': 100000000, 'far_terms': 10000000000, 'store_second': 100000000, 'far_second': 1, 'finish': 100000}


def call(kernel, outs, args, in_spaces, out_spaces, scratch=(), vmem=40 << 20, aliases=None):
    shapes = [
        pltpu.VMEM(shape, jnp.float32) if space is pltpu.VMEM else jax.ShapeDtypeStruct(shape, jnp.float32)
        for shape, space in zip(outs, out_spaces)
    ]
    out_spaces = [space or pltpu.VMEM for space in out_spaces]
    return pl.pallas_call(
        kernel,
        out_shape=shapes,
        in_specs=[pl.BlockSpec(memory_space=space) for space in in_spaces],
        out_specs=[pl.BlockSpec(memory_space=space) for space in out_spaces],
        scratch_shapes=list(scratch),
        name=kernel.__name__,
        input_output_aliases=aliases or {},
        compiler_params=pltpu.CompilerParams(vmem_limit_bytes=vmem),
        cost_estimate=pl.CostEstimate(
            flops=costs.get(kernel.__name__, 1), bytes_accessed=costs.get(kernel.__name__, 1), transcendentals=0
        ),
    )(*args)


def local(adjoint_now, adjoint_prev, forward_field, density, lame_first, shear_modulus):
    slabs = lax.axis_size("blk")
    events = lax.axis_size("event")
    cells, rows, lanes = density.shape
    steps = forward_field.shape[1]
    last = cells - 1
    band = rows // events
    plane = (rows, lanes)
    VM, SM, ANY = pltpu.VMEM, pltpu.SMEM, pl.ANY

    near = [(i, i + 1 - 2 * (i % 2)) for i in range(slabs)]
    far = [(i, (i - 1 + 2 * (i % 2)) % slabs) for i in range(slabs)]
    others = [
        [(i, (i + shift) % events) for i in range(events)] for shift in range(1, events)
    ]

    in_hbm = [
        pltpu.with_memory_space_constraint(x, pltpu.HBM)
        for x in (adjoint_now[0], adjoint_prev[0], forward_field[0], density, lame_first, shear_modulus)
    ]
    now_hbm, prev, forward_hbm, density, lame_hbm, shear_hbm = in_hbm
    now, forward = adjoint_now[0], forward_field[0]

    def where():
        return lax.rem(lax.axis_index("blk"), 2), lax.axis_index("event")

    def layer(place_ref, t):
        return t + place_ref[0] * (last - 2 * t)

    def far_slot(place_ref, n):
        return (1 - n) + place_ref[0] * (2 * n - 1)

    def near_slot(place_ref, n):
        return n + place_ref[0] * (1 - 2 * n)

    def sign(place_ref):
        return (1 - 2 * place_ref[0]).astype(jnp.float32)

    def pack(now_ref, lame_ref, shear_ref, near_ref, near_model_ref, far_ref, sem):
        place_ref = where()
        odd = place_ref[0]
        at, low = layer(place_ref, 0), odd * (cells - 2)
        copies = [
            (now_ref.at[:, pl.ds(low, 2)], far_ref.at[pl.ds(0, 3)]),
            (lame_ref.at[at], far_ref.at[3, 0]),
            (shear_ref.at[at], far_ref.at[3, 1]),
        ]
        at, low = layer(place_ref, last), (1 - odd) * (cells - 2)
        copies.append((now_ref.at[:, pl.ds(low, 2)], near_ref))
        copies.append((lame_ref.at[at], near_model_ref.at[0]))
        copies.append((shear_ref.at[at], near_model_ref.at[1]))
        started = [pltpu.make_async_copy(src, dst, sem.at[i]) for i, (src, dst) in enumerate(copies)]
        for copy in started:
            copy.start()
        for copy in started:
            copy.wait()

    near_out, near_model_out, far_out = call(
        pack,
        [(3, 2, *plane), (2, *plane), (4, 2, *plane)],
        (now_hbm, lame_hbm, shear_hbm),
        [ANY, ANY, ANY],
        [VM] * 3,
        [pltpu.SemaphoreType.DMA((6,))],
    )
    near_in = lax.ppermute(near_out, "blk", near)
    near_model_in = lax.ppermute(near_model_out, "blk", near)
    far_in = lax.ppermute(far_out, "blk", far)

    def split(place_ref, terms_ref, layers, keep_ref, send_ref):
        own = place_ref[1]
        for shift in range(events):
            target = lax.rem(own + shift, events) if shift else own
            start = pl.multiple_of(target * band, 8)
            out = send_ref.at[shift - 1] if shift else keep_ref
            for k in range(2):
                for i, t in enumerate(layers):
                    out[k, i] = terms_ref[k, t, pl.ds(start, band)]

    inner = range(3, last - 2)

    def inner_first(now_v, prev_ref, fwd_v, dens_ref, lame_v, shear_v,
        scale_v, next_v, terms_v, far_fwd_ref,
        prev_v, dens_v, normal_v, sem,
    ):
        place_ref = where()
        moves = [
            pltpu.make_async_copy(src, dst, sem.at[i])
            for i, (src, dst) in enumerate([(dens_ref, dens_v), (prev_ref, prev_v)])
        ]
        for move in moves:
            move.start()
        sigma = sign(place_ref)
        tools = difference_tools(*plane)

        def at(t):
            return layer(place_ref, t)

        def field(t):
            return (now_v[0, at(t)] * sigma, now_v[1, at(t)], now_v[2, at(t)])

        def fwd(k, t):
            return (fwd_v[k, 0, at(t)] * sigma, fwd_v[k, 1, at(t)], fwd_v[k, 2, at(t)])

        for k in range(steps):
            for b in range(3):
                far_fwd_ref[k, b] = fwd_v[k, b, at(0)]
        for t in range(1, last):
            parts = strain_parts(field(t - 1), field(t), field(t + 1), tools)
            lame, shear = lame_v[at(t)], shear_v[at(t)]
            normal = normal_stress(parts, lame, shear)
            force = cross_force(parts, normal, lame, shear, tools)
            for b in range(3):
                normal_v[b, t] = normal[b]
                next_v[b, t] = force[b]
            other = strain_parts(fwd(0, t - 1), fwd(0, t), fwd(0, t + 1), tools)
            pair = term_pair(parts, other, lame, shear)
            terms_v[0, t] = pair[0]
            terms_v[1, t] = pair[1]
        for move in moves:
            move.wait()
        for t in range(cells):
            scale_v[t] = (0.25 * step_squared) / dens_v[at(t)]
        for t in range(cells):
            for b in range(3):
                force = None
                if 0 < t < last:
                    force = next_v[b, t]
                if t < last - 1:
                    force = normal_v[b, t + 1] if force is None else force + normal_v[b, t + 1]
                if t > 1:
                    force = -normal_v[b, t - 1] if force is None else force - normal_v[b, t - 1]
                old = prev_v[b, at(t)]
                if b == 0:
                    old = old * sigma
                next_v[b, t] = 2.0 * field(t)[b] - old + scale_v[t] * force
        for t in inner:
            fields = [tuple(next_v[b, t + d] for b in range(3)) for d in (-1, 0, 1)]
            parts = strain_parts(*fields, tools)
            other = strain_parts(fwd(1, t - 1), fwd(1, t), fwd(1, t + 1), tools)
            pair = term_pair(parts, other, lame_v[at(t)], shear_v[at(t)])
            for k in range(2):
                terms_v[k, t] = terms_v[k, t] + pair[k]

    now_v, fwd_v, lame_v, shear_v = now, forward, lame_first, shear_modulus
    scale_v, next_v, terms_v, far_fwd_out = call(
        inner_first,
        [density.shape, now.shape, (2, last, *plane), (steps, 3, *plane)],
        (now, prev, forward, density, lame_first, shear_modulus),
        [VM, ANY, VM, ANY, VM, VM],
        [VM] * 4,
        [pltpu.VMEM(now.shape, jnp.float32), pltpu.VMEM(density.shape, jnp.float32),
         pltpu.VMEM((3, last, *plane), jnp.float32), pltpu.SemaphoreType.DMA((2,))],
    )

    far_fwd_in = lax.ppermute(far_fwd_out, "blk", far)

    middle = list(range(1, cells))

    def near_first(now_v, fwd_v, lame_v, shear_v, scale_v, next_v, near_ref, near_model_ref, near_next):
        place_ref = where()
        sigma = sign(place_ref)
        tools = difference_tools(*plane)

        def at(t):
            return layer(place_ref, t)

        def field(t):
            if t <= last:
                return (now_v[0, at(t)] * sigma, now_v[1, at(t)], now_v[2, at(t)])
            slot = near_slot(place_ref, t - cells)
            return (near_ref[0, slot] * sigma, near_ref[1, slot], near_ref[2, slot])

        outer = normal_stress(
            strain_parts(field(last), field(cells), field(cells + 1), tools), near_model_ref[0], near_model_ref[1]
        )
        lame, shear = lame_v[at(last)], shear_v[at(last)]
        parts = strain_parts(field(last - 1), field(last), field(cells), tools)
        normal = normal_stress(parts, lame, shear)
        force = cross_force(parts, normal, lame, shear, tools)
        for b in range(3):
            near_next[b] = next_v[b, last] + scale_v[last] * (force[b] + outer[b])
            near_next[3 + b] = next_v[b, last - 1] + scale_v[last - 1] * normal[b]
            for k in range(steps):
                near_next[6 + 3 * k + b] = fwd_v[k, b, at(last)]

    (near_next,) = call(
        near_first,
        [(6 + 3 * steps, *plane)],
        (now_v, fwd_v, lame_v, shear_v, scale_v, next_v, near_in, near_model_in),
        [VM] * 8,
        [VM],
    )
    near_next_in = lax.ppermute(near_next, "blk", near)

    def far_first(now_v, lame_v, shear_v, scale_v, next_v, far_ref, after_ref, far_next, far_after):
        place_ref = where()
        sigma = sign(place_ref)
        tools = difference_tools(*plane)

        def at(t):
            return layer(place_ref, t)

        def field(t):
            if t >= 0:
                return (now_v[0, at(t)] * sigma, now_v[1, at(t)], now_v[2, at(t)])
            slot = far_slot(place_ref, -1 - t)
            return (far_ref[0, slot] * sigma, far_ref[1, slot], far_ref[2, slot])

        outer = normal_stress(strain_parts(field(-2), field(-1), field(0), tools), far_ref[3, 0], far_ref[3, 1])
        lame, shear = lame_v[at(0)], shear_v[at(0)]
        parts = strain_parts(field(-1), field(0), field(1), tools)
        normal = normal_stress(parts, lame, shear)
        force = cross_force(parts, normal, lame, shear, tools)
        for b in range(3):
            far_next[b] = next_v[b, 0] + scale_v[0] * (force[b] - outer[b])
            far_after[b] = next_v[b, 1] - scale_v[1] * normal[b]

    far_next, far_after = call(
        far_first,
        [(3, *plane), (3, *plane)],
        (now_v, lame_v, shear_v, scale_v, next_v, far_in, near_next),
        [VM] * 7,
        [VM] * 2,
    )
    far_next_in = lax.ppermute(far_next, "blk", far)
    far_after_in = lax.ppermute(far_after, "blk", far)

    def middle_terms(now_v, fwd_v, lame_v, shear_v, next_v, near_next_v, terms_v, far_next_ref, far_after_ref, near_next_ref,
        near_ref,
        keep_ref, send_ref, total_v,
    ):
        place_ref = where()
        sigma = sign(place_ref)
        tools = difference_tools(*plane)

        def at(t):
            return layer(place_ref, t)

        def field(t):
            if t < 2:
                return tuple((far_after_ref if t else far_next_ref)[b] for b in range(3))
            if t < last - 1:
                return tuple(next_v[b, t] for b in range(3))
            if t <= last:
                return tuple(near_next_v[3 * (last - t) + b] for b in range(3))
            base = 3 * (t - cells)
            return (-near_next_ref[base], near_next_ref[base + 1], near_next_ref[base + 2])

        def fwd(k, t):
            if t <= last:
                return (fwd_v[k, 0, at(t)] * sigma, fwd_v[k, 1, at(t)], fwd_v[k, 2, at(t)])
            return (near_next_ref[6 + 3 * k] * sigma, near_next_ref[7 + 3 * k], near_next_ref[8 + 3 * k])

        def start(t):
            if t <= last:
                return (now_v[0, at(t)] * sigma, now_v[1, at(t)], now_v[2, at(t)])
            slot = near_slot(place_ref, t - cells)
            return (near_ref[0, slot] * sigma, near_ref[1, slot], near_ref[2, slot])

        for t in middle:
            lame, shear = lame_v[at(t)], shear_v[at(t)]
            if t < last:
                total = (terms_v[0, t], terms_v[1, t])
            else:
                parts = strain_parts(start(t - 1), start(t), start(t + 1), tools)
                other = strain_parts(fwd(0, t - 1), fwd(0, t), fwd(0, t + 1), tools)
                total = term_pair(parts, other, lame, shear)
            if t not in inner:
                parts = strain_parts(field(t - 1), field(t), field(t + 1), tools)
                other = strain_parts(fwd(1, t - 1), fwd(1, t), fwd(1, t + 1), tools)
                pair = term_pair(parts, other, lame, shear)
                total = (total[0] + pair[0], total[1] + pair[1])
            for k in range(2):
                total_v[k, t] = total[k]
        split(place_ref, total_v, middle, keep_ref, send_ref)

    keep_mid, send_mid = call(
        middle_terms,
        [(2, len(middle), band, lanes), (events - 1, 2, len(middle), band, lanes)],
        (now_v, fwd_v, lame_v, shear_v, next_v, near_next, terms_v, far_next, far_after, near_next_in, near_in),
        [VM] * 11,
        [VM] * 2,
        [pltpu.VMEM((2, cells, *plane), jnp.float32)],
    )
    shared_mid = [lax.ppermute(send_mid[i], "event", others[i]) for i in range(events - 1)]

    def edge_terms(now_v, fwd_v, lame_v, shear_v, far_next_ref, far_after_ref, far_ref, far_fwd_ref, after_ref,
        total_v, slope_v,
    ):
        place_ref = where()
        sigma = sign(place_ref)
        tools = difference_tools(*plane)

        def at(t):
            return layer(place_ref, t)

        def start(t):
            if t >= 0:
                return (now_v[0, at(t)] * sigma, now_v[1, at(t)], now_v[2, at(t)])
            slot = far_slot(place_ref, 0)
            return (far_ref[0, slot] * sigma, far_ref[1, slot], far_ref[2, slot])

        def field(t):
            return tuple((far_after_ref if t else far_next_ref)[b] for b in range(3))

        def fwd(k, t):
            if t < 0:
                return (far_fwd_ref[k, 0] * sigma, far_fwd_ref[k, 1], far_fwd_ref[k, 2])
            return (fwd_v[k, 0, at(t)] * sigma, fwd_v[k, 1, at(t)], fwd_v[k, 2, at(t)])

        parts = strain_parts(start(-1), start(0), start(1), tools)
        other = strain_parts(fwd(0, -1), fwd(0, 0), fwd(0, 1), tools)
        lame, shear = lame_v[at(0)], shear_v[at(0)]
        pair = term_pair(parts, other, lame, shear)
        empty = jnp.zeros(plane, jnp.float32)
        parts = strain_parts((empty, empty, empty), field(0), field(1), tools)
        other = strain_parts(fwd(1, -1), fwd(1, 0), fwd(1, 1), tools)
        rest = term_pair(parts, other, lame, shear)
        for k in range(2):
            total_v[k] = pair[k] + rest[k]
        slope_v[0] = shear * ((0.5 * time_step) * other[0] - (time_step / 6.0) * other[6])
        slope_v[1] = (0.25 * time_step) * shear * other[3]
        slope_v[2] = (0.25 * time_step) * shear * other[4]
        slope_v[3] = (0.25 * time_step) * (lame + (2.0 / 3.0) * shear) * other[6]

    total_v, slope_v = call(
        edge_terms,
        [(2, *plane), (4, *plane)],
        (now_v, fwd_v, lame_v, shear_v, far_next, far_after, far_in, far_fwd_in, keep_mid),
        [VM] * 9,
        [VM] * 2,
    )

    def far_terms(total_ref, slope_ref, far_next_in_ref, keep_ref, send_ref, total_v):
        place_ref = where()
        outer = (-far_next_in_ref[0], far_next_in_ref[1], far_next_in_ref[2])
        shear_part = total_ref[0]
        for b in range(3):
            shear_part = shear_part + slope_ref[b] * outer[b]
        total_v[0, 0] = shear_part
        total_v[1, 0] = total_ref[1] + slope_ref[3] * outer[0]
        split(place_ref, total_v, [0], keep_ref, send_ref)

    far_keep, far_send = call(
        far_terms,
        [(2, 1, band, lanes), (events - 1, 2, 1, band, lanes)],
        (total_v, slope_v, far_next_in),
        [VM] * 3,
        [VM] * 2,
        [pltpu.VMEM((2, 1, *plane), jnp.float32)],
    )
    far_shared = [lax.ppermute(far_send[i], "event", others[i]) for i in range(events - 1)]

    def second(now_v, lame_v, shear_v, scale_v, next_v, near_next_v, far_next_ref, far_after_ref, near_next_ref,
        near_model_ref, after_ref,
        final_v, face_v, normal_v, cross_v,
    ):
        place_ref = where()
        sigma = sign(place_ref)
        tools = difference_tools(*plane)

        def at(t):
            return layer(place_ref, t)

        def field(t):
            if t < 2:
                return tuple((far_after_ref if t else far_next_ref)[b] for b in range(3))
            if t < last - 1:
                return tuple(next_v[b, t] for b in range(3))
            if t <= last:
                return tuple(near_next_v[3 * (last - t) + b] for b in range(3))
            base = 3 * (t - cells)
            return (-near_next_ref[base], near_next_ref[base + 1], near_next_ref[base + 2])

        for t in range(1, cells + 1):
            parts = strain_parts(field(t - 1), field(t), field(t + 1), tools)
            if t <= last:
                lame, shear = lame_v[at(t)], shear_v[at(t)]
            else:
                lame, shear = near_model_ref[0], near_model_ref[1]
            normal = normal_stress(parts, lame, shear)
            for b in range(3):
                normal_v[b, t] = normal[b]
            if t <= last:
                force = cross_force(parts, normal, lame, shear, tools)
                for b in range(3):
                    cross_v[b, t] = force[b]
        for t in range(cells):
            for b in range(3):
                force = normal_v[b, t + 1]
                if t > 0:
                    force = force + cross_v[b, t]
                if t > 1:
                    force = force - normal_v[b, t - 1]
                old = now_v[b, at(t)]
                if b == 0:
                    old = old * sigma
                value = 2.0 * field(t)[b] - old + scale_v[t] * force
                if t < 2:
                    face_v[b, t] = value
                else:
                    final_v[b, at(t)] = value * sigma if b == 0 else value

    final_v, face_v = call(
        second,
        [now.shape, (3, 2, *plane)],
        (now_v, lame_v, shear_v, scale_v, next_v, near_next, far_next, far_after, near_next_in,
         near_model_in, far_keep),
        [VM] * 11,
        [VM] * 2,
        [pltpu.VMEM((3, cells + 1, *plane), jnp.float32), pltpu.VMEM(now.shape, jnp.float32)],
    )

    def store_second(final_v, out_ref, done_ref, sem):
        place_ref = where()
        inner = pl.ds(2 - 2 * place_ref[0], cells - 2)
        copy = pltpu.make_async_copy(final_v.at[:, inner], out_ref.at[:, inner], sem)
        copy.start()
        copy.wait()
        done_ref[...] = jnp.zeros((8, lanes), jnp.float32)

    result, done = call(
        store_second, [now.shape, (8, lanes)], (final_v,), [VM], [ANY, VM], [pltpu.SemaphoreType.DMA(())]
    )

    def far_second(lame_v, shear_v, scale_v, face_v, far_next_ref, far_after_ref, far_ref,
        far_next_in_ref, far_after_in_ref, after_ref, edge_v,
    ):
        place_ref = where()
        sigma = sign(place_ref)
        tools = difference_tools(*plane)

        def at(t):
            return layer(place_ref, t)

        def field(t):
            if t < 0:
                come = far_next_in_ref if t == -1 else far_after_in_ref
                return (-come[0], come[1], come[2])
            return tuple((far_after_ref if t else far_next_ref)[b] for b in range(3))

        outer = normal_stress(strain_parts(field(-2), field(-1), field(0), tools), far_ref[3, 0], far_ref[3, 1])
        lame, shear = lame_v[at(0)], shear_v[at(0)]
        parts = strain_parts(field(-1), field(0), field(1), tools)
        normal = normal_stress(parts, lame, shear)
        force = cross_force(parts, normal, lame, shear, tools)
        odd = place_ref[0]
        for b in range(3):
            first = face_v[b, 0] + scale_v[0] * (force[b] - outer[b])
            after = face_v[b, 1] - scale_v[1] * normal[b]
            edge_v[b, odd] = first * sigma if b == 0 else first
            edge_v[b, 1 - odd] = after * sigma if b == 0 else after

    (edge,) = call(
        far_second,
        [(3, 2, *plane)],
        (lame_v, shear_v, scale_v, face_v, far_next, far_after, far_in, far_next_in, far_after_in, done),
        [VM] * 10,
        [VM],
    )

    def finish(result_ref, edge_v, *rest):
        pieces, (out_ref, *band_refs, band_v, sem) = rest[: 2 * events], rest[2 * events :]
        place_ref = where()
        copies = [
            pltpu.make_async_copy(edge_v, out_ref.at[:, pl.ds(place_ref[0] * (cells - 2), 2)], sem.at[0])
        ]
        copies[0].start()
        for k in range(2):
            groups = (([0], pieces[:events]), (middle, pieces[events:]))
            for layers, (own, *others_parts) in groups:
                for j, t in enumerate(layers):
                    value = own[k, j]
                    for part in others_parts:
                        value = value + part[k, j]
                    band_v[k, layer(place_ref, t)] = value
            copies.append(pltpu.make_async_copy(band_v.at[k], band_refs[k], sem.at[1 + k]))
            copies[-1].start()
        for copy in copies:
            copy.wait()

    result, band_shear, band_bulk = call(
        finish,
        [now.shape, (cells, band, lanes), (cells, band, lanes)],
        (result, edge, far_keep, *far_shared, keep_mid, *shared_mid),
        [ANY] + [VM] * (1 + 2 * events),
        [ANY] * 3,
        [pltpu.VMEM((2, cells, band, lanes), jnp.float32), pltpu.SemaphoreType.DMA((3,))],
        aliases={0: 0},
    )
    return (result[None], band_shear, band_bulk)


def solution(mesh):
    in_specs = (
        P("event", None, "blk", None, None),
        P("event", None, "blk", None, None),
        P("event", None, None, "blk", None, None),
        P("blk", None, None),
        P("blk", None, None),
        P("blk", None, None),
    )
    out_specs = (
        P("event", None, "blk", None, None),
        P("blk", "event", None),
        P("blk", "event", None),
    )
    return jax.shard_map(local, mesh=mesh, in_specs=in_specs, out_specs=out_specs, check_vma=False)
```

```python
import jax
import jax.numpy as jnp
from jax import lax
from jax.experimental import pallas as pl
from jax.experimental.pallas import tpu as pltpu
from jax.sharding import PartitionSpec as P

time_step = 0.3
step_squared = time_step * time_step


def difference_tools(rows, lanes):
    row = lax.broadcasted_iota(jnp.int32, (rows, lanes), 0)
    lane = lax.broadcasted_iota(jnp.int32, (rows, lanes), 1)

    def along_rows(values):
        upper = jnp.where(row == rows - 1, 0.0, pltpu.roll(values, rows - 1, 0))
        lower = jnp.where(row == 0, 0.0, pltpu.roll(values, 1, 0))
        return upper - lower

    def along_lanes(values):
        upper = jnp.where(lane == lanes - 1, 0.0, pltpu.roll(values, lanes - 1, 1))
        lower = jnp.where(lane == 0, 0.0, pltpu.roll(values, 1, 1))
        return upper - lower

    key = lax.broadcasted_iota(jnp.int32, (3 * lanes, lanes), 0) % lanes
    out = lax.broadcasted_iota(jnp.int32, (3 * lanes, lanes), 1)
    weights = ((key == out + 1).astype(jnp.float32) - (key == out - 1).astype(jnp.float32)).astype(jnp.bfloat16)

    def along_lanes_three(fields):
        values = jnp.concatenate(fields, axis=0)
        high = values.astype(jnp.bfloat16)
        rest = values - high.astype(jnp.float32)
        middle = rest.astype(jnp.bfloat16)
        low = (rest - middle.astype(jnp.float32)).astype(jnp.bfloat16)
        parts = jnp.concatenate([high, middle, low], axis=1)
        result = jnp.dot(parts, weights, preferred_element_type=jnp.float32)
        return [result[rows * b : rows * (b + 1)] for b in range(len(fields))]

    return along_rows, along_lanes, along_lanes_three


def strain_parts(before, middle, after, tools):
    along_rows, along_lanes, along_lanes_three = tools
    first = after[0] - before[0]
    second = along_rows(middle[1])
    third = along_lanes(middle[2])
    pair_12 = (after[1] - before[1]) + along_rows(middle[0])
    pair_13 = (after[2] - before[2]) + along_lanes(middle[0])
    pair_23 = along_rows(middle[2]) + along_lanes(middle[1])
    return (first, second, third, pair_12, pair_13, pair_23, first + second + third)


def normal_stress(parts, lame, shear):
    return (2.0 * shear * parts[0] + lame * parts[6], shear * parts[3], shear * parts[4])


def cross_force(parts, normal, lame, shear, tools):
    along_rows, along_lanes, along_lanes_three = tools
    pressure = lame * parts[6]
    twice = 2.0 * shear
    s_22 = twice * parts[1] + pressure
    s_33 = twice * parts[2] + pressure
    s_23 = shear * parts[5]
    third_of = along_lanes_three((normal[2], s_23, s_33))
    return (
        along_rows(normal[1]) + third_of[0],
        along_rows(s_22) + third_of[1],
        along_rows(s_23) + third_of[2],
    )


def term_pair(parts, other, lame, shear):
    straight = parts[0] * other[0] + parts[1] * other[1] + parts[2] * other[2]
    mixed = parts[3] * other[3] + parts[4] * other[4] + parts[5] * other[5]
    traces = parts[6] * other[6]
    shear_term = shear * (
        (-0.5 * time_step) * straight - (0.25 * time_step) * mixed + (time_step / 6.0) * traces
    )
    bulk_term = (-0.25 * time_step) * (lame + (2.0 / 3.0) * shear) * traces
    return shear_term, bulk_term


costs = {'pack': 1000000000, 'inner_first': 1000000000, 'near_first': 1000000, 'far_first': 10000000000, 'middle_terms': 10000000, 'edge_terms': 10000000, 'second': 100000000, 'far_terms': 10000000000, 'store_second': 100000000, 'far_second': 1, 'finish': 100000}


def call(kernel, outs, args, in_spaces, out_spaces, scratch=(), vmem=40 << 20, aliases=None):
    shapes = [
        pltpu.VMEM(shape, jnp.float32) if space is pltpu.VMEM else jax.ShapeDtypeStruct(shape, jnp.float32)
        for shape, space in zip(outs, out_spaces)
    ]
    out_spaces = [space or pltpu.VMEM for space in out_spaces]
    return pl.pallas_call(
        kernel,
        out_shape=shapes,
        in_specs=[pl.BlockSpec(memory_space=space) for space in in_spaces],
        out_specs=[pl.BlockSpec(memory_space=space) for space in out_spaces],
        scratch_shapes=list(scratch),
        name=kernel.__name__,
        input_output_aliases=aliases or {},
        compiler_params=pltpu.CompilerParams(vmem_limit_bytes=vmem),
        cost_estimate=pl.CostEstimate(
            flops=costs.get(kernel.__name__, 1), bytes_accessed=costs.get(kernel.__name__, 1), transcendentals=0
        ),
    )(*args)


def local(adjoint_now, adjoint_prev, forward_field, density, lame_first, shear_modulus):
    slabs = lax.axis_size("blk")
    events = lax.axis_size("event")
    cells, rows, lanes = density.shape
    steps = forward_field.shape[1]
    last = cells - 1
    band = rows // events
    plane = (rows, lanes)
    VM, SM, ANY = pltpu.VMEM, pltpu.SMEM, pl.ANY

    near = [(i, i + 1 - 2 * (i % 2)) for i in range(slabs)]
    far = [(i, (i - 1 + 2 * (i % 2)) % slabs) for i in range(slabs)]
    others = [
        [(i, (i + shift) % events) for i in range(events)] for shift in range(1, events)
    ]

    in_hbm = [
        pltpu.with_memory_space_constraint(x, pltpu.HBM)
        for x in (adjoint_now[0], adjoint_prev[0], forward_field[0], density, lame_first, shear_modulus)
    ]
    now_hbm, prev, forward_hbm, density, lame_hbm, shear_hbm = in_hbm
    now, forward = adjoint_now[0], forward_field[0]

    def where():
        return lax.rem(lax.axis_index("blk"), 2), lax.axis_index("event")

    def layer(place_ref, t):
        return t + place_ref[0] * (last - 2 * t)

    def far_slot(place_ref, n):
        return (1 - n) + place_ref[0] * (2 * n - 1)

    def near_slot(place_ref, n):
        return n + place_ref[0] * (1 - 2 * n)

    def sign(place_ref):
        return (1 - 2 * place_ref[0]).astype(jnp.float32)

    def pack(now_ref, lame_ref, shear_ref, near_ref, near_model_ref, far_ref, sem):
        place_ref = where()
        odd = place_ref[0]
        at, low = layer(place_ref, 0), odd * (cells - 2)
        copies = [
            (now_ref.at[:, pl.ds(low, 2)], far_ref.at[pl.ds(0, 3)]),
            (lame_ref.at[at], far_ref.at[3, 0]),
            (shear_ref.at[at], far_ref.at[3, 1]),
        ]
        at, low = layer(place_ref, last), (1 - odd) * (cells - 2)
        copies.append((now_ref.at[:, pl.ds(low, 2)], near_ref))
        copies.append((lame_ref.at[at], near_model_ref.at[0]))
        copies.append((shear_ref.at[at], near_model_ref.at[1]))
        started = [pltpu.make_async_copy(src, dst, sem.at[i]) for i, (src, dst) in enumerate(copies)]
        for copy in started:
            copy.start()
        for copy in started:
            copy.wait()

    near_out, near_model_out, far_out = call(
        pack,
        [(3, 2, *plane), (2, *plane), (4, 2, *plane)],
        (now_hbm, lame_hbm, shear_hbm),
        [ANY, ANY, ANY],
        [VM] * 3,
        [pltpu.SemaphoreType.DMA((6,))],
    )
    near_in = lax.ppermute(near_out, "blk", near)
    near_model_in = lax.ppermute(near_model_out, "blk", near)
    far_in = lax.ppermute(far_out, "blk", far)

    def split(place_ref, terms_ref, layers, keep_ref, send_ref):
        own = place_ref[1]
        for shift in range(events):
            target = lax.rem(own + shift, events) if shift else own
            start = pl.multiple_of(target * band, 8)
            out = send_ref.at[shift - 1] if shift else keep_ref
            for k in range(2):
                for i, t in enumerate(layers):
                    out[k, i] = terms_ref[k, t, pl.ds(start, band)]

    inner = range(3, last - 2)

    def inner_first(now_v, prev_ref, fwd_v, dens_ref, lame_v, shear_v,
        scale_v, next_v, terms_v, far_fwd_ref,
        prev_v, dens_v, normal_v, sem,
    ):
        place_ref = where()
        moves = [
            pltpu.make_async_copy(src, dst, sem.at[i])
            for i, (src, dst) in enumerate([(dens_ref, dens_v), (prev_ref, prev_v)])
        ]
        for move in moves:
            move.start()
        sigma = sign(place_ref)
        tools = difference_tools(*plane)

        def at(t):
            return layer(place_ref, t)

        def field(t):
            return (now_v[0, at(t)] * sigma, now_v[1, at(t)], now_v[2, at(t)])

        def fwd(k, t):
            return (fwd_v[k, 0, at(t)] * sigma, fwd_v[k, 1, at(t)], fwd_v[k, 2, at(t)])

        for k in range(steps):
            for b in range(3):
                far_fwd_ref[k, b] = fwd_v[k, b, at(0)]
        for t in range(1, last):
            parts = strain_parts(field(t - 1), field(t), field(t + 1), tools)
            lame, shear = lame_v[at(t)], shear_v[at(t)]
            normal = normal_stress(parts, lame, shear)
            force = cross_force(parts, normal, lame, shear, tools)
            for b in range(3):
                normal_v[b, t] = normal[b]
                next_v[b, t] = force[b]
            other = strain_parts(fwd(0, t - 1), fwd(0, t), fwd(0, t + 1), tools)
            pair = term_pair(parts, other, lame, shear)
            terms_v[0, t] = pair[0]
            terms_v[1, t] = pair[1]
        for move in moves:
            move.wait()
        for t in range(cells):
            scale_v[t] = (0.25 * step_squared) / dens_v[at(t)]
        for t in range(cells):
            for b in range(3):
                force = None
                if 0 < t < last:
                    force = next_v[b, t]
                if t < last - 1:
                    force = normal_v[b, t + 1] if force is None else force + normal_v[b, t + 1]
                if t > 1:
                    force = -normal_v[b, t - 1] if force is None else force - normal_v[b, t - 1]
                old = prev_v[b, at(t)]
                if b == 0:
                    old = old * sigma
                next_v[b, t] = 2.0 * field(t)[b] - old + scale_v[t] * force
        for t in inner:
            fields = [tuple(next_v[b, t + d] for b in range(3)) for d in (-1, 0, 1)]
            parts = strain_parts(*fields, tools)
            other = strain_parts(fwd(1, t - 1), fwd(1, t), fwd(1, t + 1), tools)
            pair = term_pair(parts, other, lame_v[at(t)], shear_v[at(t)])
            for k in range(2):
                terms_v[k, t] = terms_v[k, t] + pair[k]

    now_v, fwd_v, lame_v, shear_v = now, forward, lame_first, shear_modulus
    scale_v, next_v, terms_v, far_fwd_out = call(
        inner_first,
        [density.shape, now.shape, (2, last, *plane), (steps, 3, *plane)],
        (now, prev, forward, density, lame_first, shear_modulus),
        [VM, ANY, VM, ANY, VM, VM],
        [VM] * 4,
        [pltpu.VMEM(now.shape, jnp.float32), pltpu.VMEM(density.shape, jnp.float32),
         pltpu.VMEM((3, last, *plane), jnp.float32), pltpu.SemaphoreType.DMA((2,))],
    )

    far_fwd_in = lax.ppermute(far_fwd_out, "blk", far)

    middle = list(range(1, cells))

    def near_first(now_v, fwd_v, lame_v, shear_v, scale_v, next_v, near_ref, near_model_ref, near_next):
        place_ref = where()
        sigma = sign(place_ref)
        tools = difference_tools(*plane)

        def at(t):
            return layer(place_ref, t)

        def field(t):
            if t <= last:
                return (now_v[0, at(t)] * sigma, now_v[1, at(t)], now_v[2, at(t)])
            slot = near_slot(place_ref, t - cells)
            return (near_ref[0, slot] * sigma, near_ref[1, slot], near_ref[2, slot])

        outer = normal_stress(
            strain_parts(field(last), field(cells), field(cells + 1), tools), near_model_ref[0], near_model_ref[1]
        )
        lame, shear = lame_v[at(last)], shear_v[at(last)]
        parts = strain_parts(field(last - 1), field(last), field(cells), tools)
        normal = normal_stress(parts, lame, shear)
        force = cross_force(parts, normal, lame, shear, tools)
        for b in range(3):
            near_next[b] = next_v[b, last] + scale_v[last] * (force[b] + outer[b])
            near_next[3 + b] = next_v[b, last - 1] + scale_v[last - 1] * normal[b]
            for k in range(steps):
                near_next[6 + 3 * k + b] = fwd_v[k, b, at(last)]

    (near_next,) = call(
        near_first,
        [(6 + 3 * steps, *plane)],
        (now_v, fwd_v, lame_v, shear_v, scale_v, next_v, near_in, near_model_in),
        [VM] * 8,
        [VM],
    )
    near_next_in = lax.ppermute(near_next, "blk", near)

    def far_first(now_v, lame_v, shear_v, scale_v, next_v, far_ref, after_ref, far_next, far_after):
        place_ref = where()
        sigma = sign(place_ref)
        tools = difference_tools(*plane)

        def at(t):
            return layer(place_ref, t)

        def field(t):
            if t >= 0:
                return (now_v[0, at(t)] * sigma, now_v[1, at(t)], now_v[2, at(t)])
            slot = far_slot(place_ref, -1 - t)
            return (far_ref[0, slot] * sigma, far_ref[1, slot], far_ref[2, slot])

        outer = normal_stress(strain_parts(field(-2), field(-1), field(0), tools), far_ref[3, 0], far_ref[3, 1])
        lame, shear = lame_v[at(0)], shear_v[at(0)]
        parts = strain_parts(field(-1), field(0), field(1), tools)
        normal = normal_stress(parts, lame, shear)
        force = cross_force(parts, normal, lame, shear, tools)
        for b in range(3):
            far_next[b] = next_v[b, 0] + scale_v[0] * (force[b] - outer[b])
            far_after[b] = next_v[b, 1] - scale_v[1] * normal[b]

    far_next, far_after = call(
        far_first,
        [(3, *plane), (3, *plane)],
        (now_v, lame_v, shear_v, scale_v, next_v, far_in, near_next),
        [VM] * 7,
        [VM] * 2,
    )
    far_next_in = lax.ppermute(far_next, "blk", far)
    far_after_in = lax.ppermute(far_after, "blk", far)

    def middle_terms(now_v, fwd_v, lame_v, shear_v, next_v, near_next_v, terms_v, far_next_ref, far_after_ref, near_next_ref,
        near_ref,
        keep_ref, send_ref, total_v,
    ):
        place_ref = where()
        sigma = sign(place_ref)
        tools = difference_tools(*plane)

        def at(t):
            return layer(place_ref, t)

        def field(t):
            if t < 2:
                return tuple((far_after_ref if t else far_next_ref)[b] for b in range(3))
            if t < last - 1:
                return tuple(next_v[b, t] for b in range(3))
            if t <= last:
                return tuple(near_next_v[3 * (last - t) + b] for b in range(3))
            base = 3 * (t - cells)
            return (-near_next_ref[base], near_next_ref[base + 1], near_next_ref[base + 2])

        def fwd(k, t):
            if t <= last:
                return (fwd_v[k, 0, at(t)] * sigma, fwd_v[k, 1, at(t)], fwd_v[k, 2, at(t)])
            return (near_next_ref[6 + 3 * k] * sigma, near_next_ref[7 + 3 * k], near_next_ref[8 + 3 * k])

        def start(t):
            if t <= last:
                return (now_v[0, at(t)] * sigma, now_v[1, at(t)], now_v[2, at(t)])
            slot = near_slot(place_ref, t - cells)
            return (near_ref[0, slot] * sigma, near_ref[1, slot], near_ref[2, slot])

        for t in middle:
            lame, shear = lame_v[at(t)], shear_v[at(t)]
            if t < last:
                total = (terms_v[0, t], terms_v[1, t])
            else:
                parts = strain_parts(start(t - 1), start(t), start(t + 1), tools)
                other = strain_parts(fwd(0, t - 1), fwd(0, t), fwd(0, t + 1), tools)
                total = term_pair(parts, other, lame, shear)
            if t not in inner:
                parts = strain_parts(field(t - 1), field(t), field(t + 1), tools)
                other = strain_parts(fwd(1, t - 1), fwd(1, t), fwd(1, t + 1), tools)
                pair = term_pair(parts, other, lame, shear)
                total = (total[0] + pair[0], total[1] + pair[1])
            for k in range(2):
                total_v[k, t] = total[k]
        split(place_ref, total_v, middle, keep_ref, send_ref)

    keep_mid, send_mid = call(
        middle_terms,
        [(2, len(middle), band, lanes), (events - 1, 2, len(middle), band, lanes)],
        (now_v, fwd_v, lame_v, shear_v, next_v, near_next, terms_v, far_next, far_after, near_next_in, near_in),
        [VM] * 11,
        [VM] * 2,
        [pltpu.VMEM((2, cells, *plane), jnp.float32)],
    )
    shared_mid = [lax.ppermute(send_mid[i], "event", others[i]) for i in range(events - 1)]

    def edge_terms(now_v, fwd_v, lame_v, shear_v, far_next_ref, far_after_ref, far_ref, far_fwd_ref, after_ref,
        total_v, slope_v,
    ):
        place_ref = where()
        sigma = sign(place_ref)
        tools = difference_tools(*plane)

        def at(t):
            return layer(place_ref, t)

        def start(t):
            if t >= 0:
                return (now_v[0, at(t)] * sigma, now_v[1, at(t)], now_v[2, at(t)])
            slot = far_slot(place_ref, 0)
            return (far_ref[0, slot] * sigma, far_ref[1, slot], far_ref[2, slot])

        def field(t):
            return tuple((far_after_ref if t else far_next_ref)[b] for b in range(3))

        def fwd(k, t):
            if t < 0:
                return (far_fwd_ref[k, 0] * sigma, far_fwd_ref[k, 1], far_fwd_ref[k, 2])
            return (fwd_v[k, 0, at(t)] * sigma, fwd_v[k, 1, at(t)], fwd_v[k, 2, at(t)])

        parts = strain_parts(start(-1), start(0), start(1), tools)
        other = strain_parts(fwd(0, -1), fwd(0, 0), fwd(0, 1), tools)
        lame, shear = lame_v[at(0)], shear_v[at(0)]
        pair = term_pair(parts, other, lame, shear)
        empty = jnp.zeros(plane, jnp.float32)
        parts = strain_parts((empty, empty, empty), field(0), field(1), tools)
        other = strain_parts(fwd(1, -1), fwd(1, 0), fwd(1, 1), tools)
        rest = term_pair(parts, other, lame, shear)
        for k in range(2):
            total_v[k] = pair[k] + rest[k]
        slope_v[0] = shear * ((0.5 * time_step) * other[0] - (time_step / 6.0) * other[6])
        slope_v[1] = (0.25 * time_step) * shear * other[3]
        slope_v[2] = (0.25 * time_step) * shear * other[4]
        slope_v[3] = (0.25 * time_step) * (lame + (2.0 / 3.0) * shear) * other[6]

    total_v, slope_v = call(
        edge_terms,
        [(2, *plane), (4, *plane)],
        (now_v, fwd_v, lame_v, shear_v, far_next, far_after, far_in, far_fwd_in, keep_mid),
        [VM] * 9,
        [VM] * 2,
    )

    def far_terms(total_ref, slope_ref, far_next_in_ref, keep_ref, send_ref, total_v):
        place_ref = where()
        outer = (-far_next_in_ref[0], far_next_in_ref[1], far_next_in_ref[2])
        shear_part = total_ref[0]
        for b in range(3):
            shear_part = shear_part + slope_ref[b] * outer[b]
        total_v[0, 0] = shear_part
        total_v[1, 0] = total_ref[1] + slope_ref[3] * outer[0]
        split(place_ref, total_v, [0], keep_ref, send_ref)

    far_keep, far_send = call(
        far_terms,
        [(2, 1, band, lanes), (events - 1, 2, 1, band, lanes)],
        (total_v, slope_v, far_next_in),
        [VM] * 3,
        [VM] * 2,
        [pltpu.VMEM((2, 1, *plane), jnp.float32)],
    )
    far_shared = [lax.ppermute(far_send[i], "event", others[i]) for i in range(events - 1)]

    def second(now_v, lame_v, shear_v, scale_v, next_v, near_next_v, far_next_ref, far_after_ref, near_next_ref,
        near_model_ref, after_ref,
        final_v, face_v, normal_v, cross_v,
    ):
        place_ref = where()
        sigma = sign(place_ref)
        tools = difference_tools(*plane)

        def at(t):
            return layer(place_ref, t)

        def field(t):
            if t < 2:
                return tuple((far_after_ref if t else far_next_ref)[b] for b in range(3))
            if t < last - 1:
                return tuple(next_v[b, t] for b in range(3))
            if t <= last:
                return tuple(near_next_v[3 * (last - t) + b] for b in range(3))
            base = 3 * (t - cells)
            return (-near_next_ref[base], near_next_ref[base + 1], near_next_ref[base + 2])

        for t in range(1, cells + 1):
            parts = strain_parts(field(t - 1), field(t), field(t + 1), tools)
            if t <= last:
                lame, shear = lame_v[at(t)], shear_v[at(t)]
            else:
                lame, shear = near_model_ref[0], near_model_ref[1]
            normal = normal_stress(parts, lame, shear)
            for b in range(3):
                normal_v[b, t] = normal[b]
            if t <= last:
                force = cross_force(parts, normal, lame, shear, tools)
                for b in range(3):
                    cross_v[b, t] = force[b]
        for t in range(cells):
            for b in range(3):
                force = normal_v[b, t + 1]
                if t > 0:
                    force = force + cross_v[b, t]
                if t > 1:
                    force = force - normal_v[b, t - 1]
                old = now_v[b, at(t)]
                if b == 0:
                    old = old * sigma
                value = 2.0 * field(t)[b] - old + scale_v[t] * force
                if t < 2:
                    face_v[b, t] = value
                else:
                    final_v[b, at(t)] = value * sigma if b == 0 else value

    final_v, face_v = call(
        second,
        [now.shape, (3, 2, *plane)],
        (now_v, lame_v, shear_v, scale_v, next_v, near_next, far_next, far_after, near_next_in,
         near_model_in, far_keep),
        [VM] * 11,
        [VM] * 2,
        [pltpu.VMEM((3, cells + 1, *plane), jnp.float32), pltpu.VMEM(now.shape, jnp.float32)],
    )

    def store_second(final_v, out_ref, sem):
        place_ref = where()
        inner = pl.ds(2 - 2 * place_ref[0], cells - 2)
        copy = pltpu.make_async_copy(final_v.at[:, inner], out_ref.at[:, inner], sem)
        copy.start()
        copy.wait()

    (result,) = call(
        store_second, [now.shape], (final_v,), [VM], [ANY], [pltpu.SemaphoreType.DMA(())]
    )

    def far_second(result_ref, lame_v, shear_v, scale_v, face_v, far_next_ref, far_after_ref, far_ref,
        far_next_in_ref, far_after_in_ref, out_ref, done_ref, edge_v, sem,
    ):
        place_ref = where()
        sigma = sign(place_ref)
        tools = difference_tools(*plane)

        def at(t):
            return layer(place_ref, t)

        def field(t):
            if t < 0:
                come = far_next_in_ref if t == -1 else far_after_in_ref
                return (-come[0], come[1], come[2])
            return tuple((far_after_ref if t else far_next_ref)[b] for b in range(3))

        outer = normal_stress(strain_parts(field(-2), field(-1), field(0), tools), far_ref[3, 0], far_ref[3, 1])
        lame, shear = lame_v[at(0)], shear_v[at(0)]
        parts = strain_parts(field(-1), field(0), field(1), tools)
        normal = normal_stress(parts, lame, shear)
        force = cross_force(parts, normal, lame, shear, tools)
        odd = place_ref[0]
        for b in range(3):
            first = face_v[b, 0] + scale_v[0] * (force[b] - outer[b])
            after = face_v[b, 1] - scale_v[1] * normal[b]
            edge_v[b, odd] = first * sigma if b == 0 else first
            edge_v[b, 1 - odd] = after * sigma if b == 0 else after
        copy = pltpu.make_async_copy(edge_v, out_ref.at[:, pl.ds(odd * (cells - 2), 2)], sem)
        copy.start()
        done_ref[...] = jnp.zeros((8, lanes), jnp.float32)
        copy.wait()

    result, done = call(
        far_second,
        [now.shape, (8, lanes)],
        (result, lame_v, shear_v, scale_v, face_v, far_next, far_after, far_in, far_next_in, far_after_in),
        [ANY] + [VM] * 9,
        [ANY, VM],
        [pltpu.VMEM((3, 2, *plane), jnp.float32), pltpu.SemaphoreType.DMA(())],
        aliases={0: 0},
    )

    def finish(after_ref, *rest):
        pieces, (*band_refs, band_v, sem) = rest[: 2 * events], rest[2 * events :]
        place_ref = where()
        copies = []
        for k in range(2):
            groups = (([0], pieces[:events]), (middle, pieces[events:]))
            for layers, (own, *others_parts) in groups:
                for j, t in enumerate(layers):
                    value = own[k, j]
                    for part in others_parts:
                        value = value + part[k, j]
                    band_v[k, layer(place_ref, t)] = value
            copies.append(pltpu.make_async_copy(band_v.at[k], band_refs[k], sem.at[k]))
            copies[-1].start()
        for copy in copies:
            copy.wait()

    band_shear, band_bulk = call(
        finish,
        [(cells, band, lanes)] * 2,
        (done, far_keep, *far_shared, keep_mid, *shared_mid),
        [VM] * (1 + 2 * events),
        [ANY] * 2,
        [pltpu.VMEM((2, cells, band, lanes), jnp.float32), pltpu.SemaphoreType.DMA((2,))],
    )
    return (result[None], band_shear, band_bulk)


def solution(mesh):
    in_specs = (
        P("event", None, "blk", None, None),
        P("event", None, "blk", None, None),
        P("event", None, None, "blk", None, None),
        P("blk", None, None),
        P("blk", None, None),
        P("blk", None, None),
    )
    out_specs = (
        P("event", None, "blk", None, None),
        P("blk", "event", None),
        P("blk", "event", None),
    )
    return jax.shard_map(local, mesh=mesh, in_specs=in_specs, out_specs=out_specs, check_vma=False)
```

```python
import jax
import jax.numpy as jnp
from jax import lax
from jax.experimental import pallas as pl
from jax.experimental.pallas import tpu as pltpu
from jax.sharding import PartitionSpec as P

time_step = 0.3
step_squared = time_step * time_step


def difference_tools(rows, lanes):
    row = lax.broadcasted_iota(jnp.int32, (rows, lanes), 0)
    lane = lax.broadcasted_iota(jnp.int32, (rows, lanes), 1)

    def along_rows(values):
        upper = jnp.where(row == rows - 1, 0.0, pltpu.roll(values, rows - 1, 0))
        lower = jnp.where(row == 0, 0.0, pltpu.roll(values, 1, 0))
        return upper - lower

    def along_lanes(values):
        upper = jnp.where(lane == lanes - 1, 0.0, pltpu.roll(values, lanes - 1, 1))
        lower = jnp.where(lane == 0, 0.0, pltpu.roll(values, 1, 1))
        return upper - lower

    key = lax.broadcasted_iota(jnp.int32, (3 * lanes, lanes), 0) % lanes
    out = lax.broadcasted_iota(jnp.int32, (3 * lanes, lanes), 1)
    weights = ((key == out + 1).astype(jnp.float32) - (key == out - 1).astype(jnp.float32)).astype(jnp.bfloat16)

    def along_lanes_three(fields):
        values = jnp.concatenate(fields, axis=0)
        high = values.astype(jnp.bfloat16)
        rest = values - high.astype(jnp.float32)
        middle = rest.astype(jnp.bfloat16)
        low = (rest - middle.astype(jnp.float32)).astype(jnp.bfloat16)
        parts = jnp.concatenate([high, middle, low], axis=1)
        result = jnp.dot(parts, weights, preferred_element_type=jnp.float32)
        return [result[rows * b : rows * (b + 1)] for b in range(len(fields))]

    return along_rows, along_lanes, along_lanes_three


def strain_parts(before, middle, after, tools):
    along_rows, along_lanes, along_lanes_three = tools
    first = after[0] - before[0]
    second = along_rows(middle[1])
    third = along_lanes(middle[2])
    pair_12 = (after[1] - before[1]) + along_rows(middle[0])
    pair_13 = (after[2] - before[2]) + along_lanes(middle[0])
    pair_23 = along_rows(middle[2]) + along_lanes(middle[1])
    return (first, second, third, pair_12, pair_13, pair_23, first + second + third)


def normal_stress(parts, lame, shear):
    return (2.0 * shear * parts[0] + lame * parts[6], shear * parts[3], shear * parts[4])


def cross_force(parts, normal, lame, shear, tools, matrix=True):
    along_rows, along_lanes, along_lanes_three = tools
    pressure = lame * parts[6]
    twice = 2.0 * shear
    s_22 = twice * parts[1] + pressure
    s_33 = twice * parts[2] + pressure
    s_23 = shear * parts[5]
    fields = (normal[2], s_23, s_33)
    third_of = along_lanes_three(fields) if matrix else [along_lanes(field) for field in fields]
    return (
        along_rows(normal[1]) + third_of[0],
        along_rows(s_22) + third_of[1],
        along_rows(s_23) + third_of[2],
    )


def term_pair(parts, other, lame, shear):
    straight = parts[0] * other[0] + parts[1] * other[1] + parts[2] * other[2]
    mixed = parts[3] * other[3] + parts[4] * other[4] + parts[5] * other[5]
    traces = parts[6] * other[6]
    shear_term = shear * (
        (-0.5 * time_step) * straight - (0.25 * time_step) * mixed + (time_step / 6.0) * traces
    )
    bulk_term = (-0.25 * time_step) * (lame + (2.0 / 3.0) * shear) * traces
    return shear_term, bulk_term


costs = {'pack': 1000000000, 'inner_first': 1000000000, 'near_first': 1000000, 'far_first': 10000000000, 'middle_terms': 10000000, 'edge_terms': 10000000, 'second': 100000000, 'far_terms': 10000000000, 'store_second': 100000000, 'far_second': 1, 'finish': 100000}


def call(kernel, outs, args, in_spaces, out_spaces, scratch=(), vmem=40 << 20, aliases=None):
    shapes = [
        pltpu.VMEM(shape, jnp.float32) if space is pltpu.VMEM else jax.ShapeDtypeStruct(shape, jnp.float32)
        for shape, space in zip(outs, out_spaces)
    ]
    out_spaces = [space or pltpu.VMEM for space in out_spaces]
    return pl.pallas_call(
        kernel,
        out_shape=shapes,
        in_specs=[pl.BlockSpec(memory_space=space) for space in in_spaces],
        out_specs=[pl.BlockSpec(memory_space=space) for space in out_spaces],
        scratch_shapes=list(scratch),
        name=kernel.__name__,
        input_output_aliases=aliases or {},
        compiler_params=pltpu.CompilerParams(vmem_limit_bytes=vmem),
        cost_estimate=pl.CostEstimate(
            flops=costs.get(kernel.__name__, 1), bytes_accessed=costs.get(kernel.__name__, 1), transcendentals=0
        ),
    )(*args)


def local(adjoint_now, adjoint_prev, forward_field, density, lame_first, shear_modulus):
    slabs = lax.axis_size("blk")
    events = lax.axis_size("event")
    cells, rows, lanes = density.shape
    steps = forward_field.shape[1]
    last = cells - 1
    band = rows // events
    plane = (rows, lanes)
    VM, SM, ANY = pltpu.VMEM, pltpu.SMEM, pl.ANY

    near = [(i, i + 1 - 2 * (i % 2)) for i in range(slabs)]
    far = [(i, (i - 1 + 2 * (i % 2)) % slabs) for i in range(slabs)]
    others = [
        [(i, (i + shift) % events) for i in range(events)] for shift in range(1, events)
    ]

    in_hbm = [
        pltpu.with_memory_space_constraint(x, pltpu.HBM)
        for x in (adjoint_now[0], adjoint_prev[0], forward_field[0], density, lame_first, shear_modulus)
    ]
    now_hbm, prev, forward_hbm, density, lame_hbm, shear_hbm = in_hbm
    now, forward = adjoint_now[0], forward_field[0]

    def where():
        return lax.rem(lax.axis_index("blk"), 2), lax.axis_index("event")

    def layer(place_ref, t):
        return t + place_ref[0] * (last - 2 * t)

    def far_slot(place_ref, n):
        return (1 - n) + place_ref[0] * (2 * n - 1)

    def near_slot(place_ref, n):
        return n + place_ref[0] * (1 - 2 * n)

    def sign(place_ref):
        return (1 - 2 * place_ref[0]).astype(jnp.float32)

    def pack(now_ref, lame_ref, shear_ref, near_ref, near_model_ref, far_ref, sem):
        place_ref = where()
        odd = place_ref[0]
        at, low = layer(place_ref, 0), odd * (cells - 2)
        copies = [
            (now_ref.at[:, pl.ds(low, 2)], far_ref.at[pl.ds(0, 3)]),
            (lame_ref.at[at], far_ref.at[3, 0]),
            (shear_ref.at[at], far_ref.at[3, 1]),
        ]
        at, low = layer(place_ref, last), (1 - odd) * (cells - 2)
        copies.append((now_ref.at[:, pl.ds(low, 2)], near_ref))
        copies.append((lame_ref.at[at], near_model_ref.at[0]))
        copies.append((shear_ref.at[at], near_model_ref.at[1]))
        started = [pltpu.make_async_copy(src, dst, sem.at[i]) for i, (src, dst) in enumerate(copies)]
        for copy in started:
            copy.start()
        for copy in started:
            copy.wait()

    near_out, near_model_out, far_out = call(
        pack,
        [(3, 2, *plane), (2, *plane), (4, 2, *plane)],
        (now_hbm, lame_hbm, shear_hbm),
        [ANY, ANY, ANY],
        [VM] * 3,
        [pltpu.SemaphoreType.DMA((6,))],
    )
    near_in = lax.ppermute(near_out, "blk", near)
    near_model_in = lax.ppermute(near_model_out, "blk", near)
    far_in = lax.ppermute(far_out, "blk", far)

    def split(place_ref, terms_ref, layers, keep_ref, send_ref):
        own = place_ref[1]
        for shift in range(events):
            target = lax.rem(own + shift, events) if shift else own
            start = pl.multiple_of(target * band, 8)
            out = send_ref.at[shift - 1] if shift else keep_ref
            for k in range(2):
                for i, t in enumerate(layers):
                    out[k, i] = terms_ref[k, t, pl.ds(start, band)]

    inner = range(3, last - 2)

    def inner_first(now_v, prev_ref, fwd_v, dens_ref, lame_v, shear_v,
        scale_v, next_v, terms_v, far_fwd_ref,
        prev_v, dens_v, normal_v, sem,
    ):
        place_ref = where()
        moves = [
            pltpu.make_async_copy(src, dst, sem.at[i])
            for i, (src, dst) in enumerate([(dens_ref, dens_v), (prev_ref, prev_v)])
        ]
        for move in moves:
            move.start()
        sigma = sign(place_ref)
        tools = difference_tools(*plane)

        def at(t):
            return layer(place_ref, t)

        def field(t):
            return (now_v[0, at(t)] * sigma, now_v[1, at(t)], now_v[2, at(t)])

        def fwd(k, t):
            return (fwd_v[k, 0, at(t)] * sigma, fwd_v[k, 1, at(t)], fwd_v[k, 2, at(t)])

        for k in range(steps):
            for b in range(3):
                far_fwd_ref[k, b] = fwd_v[k, b, at(0)]
        for t in range(1, last):
            parts = strain_parts(field(t - 1), field(t), field(t + 1), tools)
            lame, shear = lame_v[at(t)], shear_v[at(t)]
            normal = normal_stress(parts, lame, shear)
            force = cross_force(parts, normal, lame, shear, tools)
            for b in range(3):
                normal_v[b, t] = normal[b]
                next_v[b, t] = force[b]
            other = strain_parts(fwd(0, t - 1), fwd(0, t), fwd(0, t + 1), tools)
            pair = term_pair(parts, other, lame, shear)
            terms_v[0, t] = pair[0]
            terms_v[1, t] = pair[1]
        for move in moves:
            move.wait()
        for t in range(cells):
            scale_v[t] = (0.25 * step_squared) / dens_v[at(t)]
        for t in range(cells):
            for b in range(3):
                force = None
                if 0 < t < last:
                    force = next_v[b, t]
                if t < last - 1:
                    force = normal_v[b, t + 1] if force is None else force + normal_v[b, t + 1]
                if t > 1:
                    force = -normal_v[b, t - 1] if force is None else force - normal_v[b, t - 1]
                old = prev_v[b, at(t)]
                if b == 0:
                    old = old * sigma
                next_v[b, t] = 2.0 * field(t)[b] - old + scale_v[t] * force
        for t in inner:
            fields = [tuple(next_v[b, t + d] for b in range(3)) for d in (-1, 0, 1)]
            parts = strain_parts(*fields, tools)
            other = strain_parts(fwd(1, t - 1), fwd(1, t), fwd(1, t + 1), tools)
            pair = term_pair(parts, other, lame_v[at(t)], shear_v[at(t)])
            for k in range(2):
                terms_v[k, t] = terms_v[k, t] + pair[k]

    now_v, fwd_v, lame_v, shear_v = now, forward, lame_first, shear_modulus
    scale_v, next_v, terms_v, far_fwd_out = call(
        inner_first,
        [density.shape, now.shape, (2, last, *plane), (steps, 3, *plane)],
        (now, prev, forward, density, lame_first, shear_modulus),
        [VM, ANY, VM, ANY, VM, VM],
        [VM] * 4,
        [pltpu.VMEM(now.shape, jnp.float32), pltpu.VMEM(density.shape, jnp.float32),
         pltpu.VMEM((3, last, *plane), jnp.float32), pltpu.SemaphoreType.DMA((2,))],
    )

    far_fwd_in = lax.ppermute(far_fwd_out, "blk", far)

    middle = list(range(1, cells))

    def near_first(now_v, fwd_v, lame_v, shear_v, scale_v, next_v, near_ref, near_model_ref, near_next):
        place_ref = where()
        sigma = sign(place_ref)
        tools = difference_tools(*plane)

        def at(t):
            return layer(place_ref, t)

        def field(t):
            if t <= last:
                return (now_v[0, at(t)] * sigma, now_v[1, at(t)], now_v[2, at(t)])
            slot = near_slot(place_ref, t - cells)
            return (near_ref[0, slot] * sigma, near_ref[1, slot], near_ref[2, slot])

        outer = normal_stress(
            strain_parts(field(last), field(cells), field(cells + 1), tools), near_model_ref[0], near_model_ref[1]
        )
        lame, shear = lame_v[at(last)], shear_v[at(last)]
        parts = strain_parts(field(last - 1), field(last), field(cells), tools)
        normal = normal_stress(parts, lame, shear)
        force = cross_force(parts, normal, lame, shear, tools, False)
        for b in range(3):
            near_next[b] = next_v[b, last] + scale_v[last] * (force[b] + outer[b])
            near_next[3 + b] = next_v[b, last - 1] + scale_v[last - 1] * normal[b]
            for k in range(steps):
                near_next[6 + 3 * k + b] = fwd_v[k, b, at(last)]

    (near_next,) = call(
        near_first,
        [(6 + 3 * steps, *plane)],
        (now_v, fwd_v, lame_v, shear_v, scale_v, next_v, near_in, near_model_in),
        [VM] * 8,
        [VM],
    )
    near_next_in = lax.ppermute(near_next, "blk", near)

    def far_first(now_v, lame_v, shear_v, scale_v, next_v, far_ref, after_ref, far_next, far_after):
        place_ref = where()
        sigma = sign(place_ref)
        tools = difference_tools(*plane)

        def at(t):
            return layer(place_ref, t)

        def field(t):
            if t >= 0:
                return (now_v[0, at(t)] * sigma, now_v[1, at(t)], now_v[2, at(t)])
            slot = far_slot(place_ref, -1 - t)
            return (far_ref[0, slot] * sigma, far_ref[1, slot], far_ref[2, slot])

        outer = normal_stress(strain_parts(field(-2), field(-1), field(0), tools), far_ref[3, 0], far_ref[3, 1])
        lame, shear = lame_v[at(0)], shear_v[at(0)]
        parts = strain_parts(field(-1), field(0), field(1), tools)
        normal = normal_stress(parts, lame, shear)
        force = cross_force(parts, normal, lame, shear, tools, False)
        for b in range(3):
            far_next[b] = next_v[b, 0] + scale_v[0] * (force[b] - outer[b])
            far_after[b] = next_v[b, 1] - scale_v[1] * normal[b]

    far_next, far_after = call(
        far_first,
        [(3, *plane), (3, *plane)],
        (now_v, lame_v, shear_v, scale_v, next_v, far_in, near_next),
        [VM] * 7,
        [VM] * 2,
    )
    far_next_in = lax.ppermute(far_next, "blk", far)
    far_after_in = lax.ppermute(far_after, "blk", far)

    def middle_terms(now_v, fwd_v, lame_v, shear_v, next_v, near_next_v, terms_v, far_next_ref, far_after_ref, near_next_ref,
        near_ref,
        keep_ref, send_ref, total_v,
    ):
        place_ref = where()
        sigma = sign(place_ref)
        tools = difference_tools(*plane)

        def at(t):
            return layer(place_ref, t)

        def field(t):
            if t < 2:
                return tuple((far_after_ref if t else far_next_ref)[b] for b in range(3))
            if t < last - 1:
                return tuple(next_v[b, t] for b in range(3))
            if t <= last:
                return tuple(near_next_v[3 * (last - t) + b] for b in range(3))
            base = 3 * (t - cells)
            return (-near_next_ref[base], near_next_ref[base + 1], near_next_ref[base + 2])

        def fwd(k, t):
            if t <= last:
                return (fwd_v[k, 0, at(t)] * sigma, fwd_v[k, 1, at(t)], fwd_v[k, 2, at(t)])
            return (near_next_ref[6 + 3 * k] * sigma, near_next_ref[7 + 3 * k], near_next_ref[8 + 3 * k])

        def start(t):
            if t <= last:
                return (now_v[0, at(t)] * sigma, now_v[1, at(t)], now_v[2, at(t)])
            slot = near_slot(place_ref, t - cells)
            return (near_ref[0, slot] * sigma, near_ref[1, slot], near_ref[2, slot])

        for t in middle:
            lame, shear = lame_v[at(t)], shear_v[at(t)]
            if t < last:
                total = (terms_v[0, t], terms_v[1, t])
            else:
                parts = strain_parts(start(t - 1), start(t), start(t + 1), tools)
                other = strain_parts(fwd(0, t - 1), fwd(0, t), fwd(0, t + 1), tools)
                total = term_pair(parts, other, lame, shear)
            if t not in inner:
                parts = strain_parts(field(t - 1), field(t), field(t + 1), tools)
                other = strain_parts(fwd(1, t - 1), fwd(1, t), fwd(1, t + 1), tools)
                pair = term_pair(parts, other, lame, shear)
                total = (total[0] + pair[0], total[1] + pair[1])
            for k in range(2):
                total_v[k, t] = total[k]
        split(place_ref, total_v, middle, keep_ref, send_ref)

    keep_mid, send_mid = call(
        middle_terms,
        [(2, len(middle), band, lanes), (events - 1, 2, len(middle), band, lanes)],
        (now_v, fwd_v, lame_v, shear_v, next_v, near_next, terms_v, far_next, far_after, near_next_in, near_in),
        [VM] * 11,
        [VM] * 2,
        [pltpu.VMEM((2, cells, *plane), jnp.float32)],
    )
    shared_mid = [lax.ppermute(send_mid[i], "event", others[i]) for i in range(events - 1)]

    def edge_terms(now_v, fwd_v, lame_v, shear_v, far_next_ref, far_after_ref, far_ref, far_fwd_ref, after_ref,
        total_v, slope_v,
    ):
        place_ref = where()
        sigma = sign(place_ref)
        tools = difference_tools(*plane)

        def at(t):
            return layer(place_ref, t)

        def start(t):
            if t >= 0:
                return (now_v[0, at(t)] * sigma, now_v[1, at(t)], now_v[2, at(t)])
            slot = far_slot(place_ref, 0)
            return (far_ref[0, slot] * sigma, far_ref[1, slot], far_ref[2, slot])

        def field(t):
            return tuple((far_after_ref if t else far_next_ref)[b] for b in range(3))

        def fwd(k, t):
            if t < 0:
                return (far_fwd_ref[k, 0] * sigma, far_fwd_ref[k, 1], far_fwd_ref[k, 2])
            return (fwd_v[k, 0, at(t)] * sigma, fwd_v[k, 1, at(t)], fwd_v[k, 2, at(t)])

        parts = strain_parts(start(-1), start(0), start(1), tools)
        other = strain_parts(fwd(0, -1), fwd(0, 0), fwd(0, 1), tools)
        lame, shear = lame_v[at(0)], shear_v[at(0)]
        pair = term_pair(parts, other, lame, shear)
        empty = jnp.zeros(plane, jnp.float32)
        parts = strain_parts((empty, empty, empty), field(0), field(1), tools)
        other = strain_parts(fwd(1, -1), fwd(1, 0), fwd(1, 1), tools)
        rest = term_pair(parts, other, lame, shear)
        for k in range(2):
            total_v[k] = pair[k] + rest[k]
        slope_v[0] = shear * ((0.5 * time_step) * other[0] - (time_step / 6.0) * other[6])
        slope_v[1] = (0.25 * time_step) * shear * other[3]
        slope_v[2] = (0.25 * time_step) * shear * other[4]
        slope_v[3] = (0.25 * time_step) * (lame + (2.0 / 3.0) * shear) * other[6]

    total_v, slope_v = call(
        edge_terms,
        [(2, *plane), (4, *plane)],
        (now_v, fwd_v, lame_v, shear_v, far_next, far_after, far_in, far_fwd_in, keep_mid),
        [VM] * 9,
        [VM] * 2,
    )

    def far_terms(total_ref, slope_ref, far_next_in_ref, keep_ref, send_ref, total_v):
        place_ref = where()
        outer = (-far_next_in_ref[0], far_next_in_ref[1], far_next_in_ref[2])
        shear_part = total_ref[0]
        for b in range(3):
            shear_part = shear_part + slope_ref[b] * outer[b]
        total_v[0, 0] = shear_part
        total_v[1, 0] = total_ref[1] + slope_ref[3] * outer[0]
        split(place_ref, total_v, [0], keep_ref, send_ref)

    far_keep, far_send = call(
        far_terms,
        [(2, 1, band, lanes), (events - 1, 2, 1, band, lanes)],
        (total_v, slope_v, far_next_in),
        [VM] * 3,
        [VM] * 2,
        [pltpu.VMEM((2, 1, *plane), jnp.float32)],
    )
    far_shared = [lax.ppermute(far_send[i], "event", others[i]) for i in range(events - 1)]

    def second(now_v, lame_v, shear_v, scale_v, next_v, near_next_v, far_next_ref, far_after_ref, near_next_ref,
        near_model_ref, after_ref,
        final_v, face_v, normal_v, cross_v,
    ):
        place_ref = where()
        sigma = sign(place_ref)
        tools = difference_tools(*plane)

        def at(t):
            return layer(place_ref, t)

        def field(t):
            if t < 2:
                return tuple((far_after_ref if t else far_next_ref)[b] for b in range(3))
            if t < last - 1:
                return tuple(next_v[b, t] for b in range(3))
            if t <= last:
                return tuple(near_next_v[3 * (last - t) + b] for b in range(3))
            base = 3 * (t - cells)
            return (-near_next_ref[base], near_next_ref[base + 1], near_next_ref[base + 2])

        for t in range(1, cells + 1):
            parts = strain_parts(field(t - 1), field(t), field(t + 1), tools)
            if t <= last:
                lame, shear = lame_v[at(t)], shear_v[at(t)]
            else:
                lame, shear = near_model_ref[0], near_model_ref[1]
            normal = normal_stress(parts, lame, shear)
            for b in range(3):
                normal_v[b, t] = normal[b]
            if t <= last:
                force = cross_force(parts, normal, lame, shear, tools)
                for b in range(3):
                    cross_v[b, t] = force[b]
        for t in range(cells):
            for b in range(3):
                force = normal_v[b, t + 1]
                if t > 0:
                    force = force + cross_v[b, t]
                if t > 1:
                    force = force - normal_v[b, t - 1]
                old = now_v[b, at(t)]
                if b == 0:
                    old = old * sigma
                value = 2.0 * field(t)[b] - old + scale_v[t] * force
                if t < 2:
                    face_v[b, t] = value
                else:
                    final_v[b, at(t)] = value * sigma if b == 0 else value

    final_v, face_v = call(
        second,
        [now.shape, (3, 2, *plane)],
        (now_v, lame_v, shear_v, scale_v, next_v, near_next, far_next, far_after, near_next_in,
         near_model_in, far_keep),
        [VM] * 11,
        [VM] * 2,
        [pltpu.VMEM((3, cells + 1, *plane), jnp.float32), pltpu.VMEM(now.shape, jnp.float32)],
    )

    def store_second(final_v, out_ref, sem):
        place_ref = where()
        inner = pl.ds(2 - 2 * place_ref[0], cells - 2)
        copy = pltpu.make_async_copy(final_v.at[:, inner], out_ref.at[:, inner], sem)
        copy.start()
        copy.wait()

    (result,) = call(
        store_second, [now.shape], (final_v,), [VM], [ANY], [pltpu.SemaphoreType.DMA(())]
    )

    def far_second(result_ref, lame_v, shear_v, scale_v, face_v, far_next_ref, far_after_ref, far_ref,
        far_next_in_ref, far_after_in_ref, out_ref, done_ref, edge_v, sem,
    ):
        place_ref = where()
        sigma = sign(place_ref)
        tools = difference_tools(*plane)

        def at(t):
            return layer(place_ref, t)

        def field(t):
            if t < 0:
                come = far_next_in_ref if t == -1 else far_after_in_ref
                return (-come[0], come[1], come[2])
            return tuple((far_after_ref if t else far_next_ref)[b] for b in range(3))

        outer = normal_stress(strain_parts(field(-2), field(-1), field(0), tools), far_ref[3, 0], far_ref[3, 1])
        lame, shear = lame_v[at(0)], shear_v[at(0)]
        parts = strain_parts(field(-1), field(0), field(1), tools)
        normal = normal_stress(parts, lame, shear)
        force = cross_force(parts, normal, lame, shear, tools)
        odd = place_ref[0]
        for b in range(3):
            first = face_v[b, 0] + scale_v[0] * (force[b] - outer[b])
            after = face_v[b, 1] - scale_v[1] * normal[b]
            edge_v[b, odd] = first * sigma if b == 0 else first
            edge_v[b, 1 - odd] = after * sigma if b == 0 else after
        copy = pltpu.make_async_copy(edge_v, out_ref.at[:, pl.ds(odd * (cells - 2), 2)], sem)
        copy.start()
        done_ref[...] = jnp.zeros((8, lanes), jnp.float32)
        copy.wait()

    result, done = call(
        far_second,
        [now.shape, (8, lanes)],
        (result, lame_v, shear_v, scale_v, face_v, far_next, far_after, far_in, far_next_in, far_after_in),
        [ANY] + [VM] * 9,
        [ANY, VM],
        [pltpu.VMEM((3, 2, *plane), jnp.float32), pltpu.SemaphoreType.DMA(())],
        aliases={0: 0},
    )

    def finish(after_ref, *rest):
        pieces, (*band_refs, band_v, sem) = rest[: 2 * events], rest[2 * events :]
        place_ref = where()
        copies = []
        for k in range(2):
            groups = (([0], pieces[:events]), (middle, pieces[events:]))
            for layers, (own, *others_parts) in groups:
                for j, t in enumerate(layers):
                    value = own[k, j]
                    for part in others_parts:
                        value = value + part[k, j]
                    band_v[k, layer(place_ref, t)] = value
            copies.append(pltpu.make_async_copy(band_v.at[k], band_refs[k], sem.at[k]))
            copies[-1].start()
        for copy in copies:
            copy.wait()

    band_shear, band_bulk = call(
        finish,
        [(cells, band, lanes)] * 2,
        (done, far_keep, *far_shared, keep_mid, *shared_mid),
        [VM] * (1 + 2 * events),
        [ANY] * 2,
        [pltpu.VMEM((2, cells, band, lanes), jnp.float32), pltpu.SemaphoreType.DMA((2,))],
    )
    return (result[None], band_shear, band_bulk)


def solution(mesh):
    in_specs = (
        P("event", None, "blk", None, None),
        P("event", None, "blk", None, None),
        P("event", None, None, "blk", None, None),
        P("blk", None, None),
        P("blk", None, None),
        P("blk", None, None),
    )
    out_specs = (
        P("event", None, "blk", None, None),
        P("blk", "event", None),
        P("blk", "event", None),
    )
    return jax.shard_map(local, mesh=mesh, in_specs=in_specs, out_specs=out_specs, check_vma=False)
```
